128 devices in a mesh: ctx: 16 (over x, y_hi, core), tp: 8 (over z, y_lo).
Axes of the slice: x: 4, y: 4 (y_hi: 2, y_lo: 2; y = y_hi * 2 + y_lo), z: 4, core: 2. Of those that a mesh axis runs over, the one named last changes fastest.
Arguments:
- tokens: bfloat16 [8192, 1024], P(('ctx', 'tp')), may hold values from -6 to 6
- cotangent: bfloat16 [8192, 1024], P(('ctx', 'tp')), may hold values from -6 to 6
- positions: int32 [8192], replicated, may hold values from 0 to 16382, as said below
- span_order: int32 [32], replicated, may hold values from 0 to 31, each once
- first_gain: float32 [1024], replicated, may hold values from 0.25 to 1.75
- w_query: bfloat16 [1024, 1024], P(None, 'tp'), may hold values from -0.1875 to 0.1875
- w_key: bfloat16 [1024, 512], P(None, 'tp'), may hold values from -0.1875 to 0.1875
- w_value: bfloat16 [1024, 512], P(None, 'tp'), may hold values from -0.1875 to 0.1875
- query_gain: float32 [64], replicated, may hold values from 0.25 to 1.75
- key_gain: float32 [64], replicated, may hold values from 0.25 to 1.75
- w_out: bfloat16 [1024, 1024], P('tp'), may hold values from -1.5 to 1.5
- second_gain: float32 [1024], replicated, may hold values from 0.25 to 1.75
- w_gate: bfloat16 [1024, 4608], P(None, 'tp'), may hold values from -0.1875 to 0.1875
- w_up: bfloat16 [1024, 4608], P(None, 'tp'), may hold values from -0.1875 to 0.1875
- w_down: bfloat16 [4608, 1024], P('tp'), may hold values from -0.09375 to 0.09375
Outputs:
- block_out: bfloat16 [8192, 1024], P(('ctx', 'tp'))
- grad_tokens: bfloat16 [8192, 1024], P(('ctx', 'tp'))
- grad_first_gain: float32 [1024], replicated
- grad_w_query: float32 [1024, 1024], P('ctx', 'tp')
- grad_w_key: float32 [1024, 512], P('ctx', 'tp')
- grad_w_value: float32 [1024, 512], P('ctx', 'tp')
- grad_query_gain: float32 [64], replicated
- grad_key_gain: float32 [64], replicated
- grad_w_out: float32 [1024, 1024], P('tp', 'ctx')
- grad_second_gain: float32 [1024], replicated
- grad_w_gate: float32 [1024, 4608], P('ctx', 'tp')
- grad_w_up: float32 [1024, 4608], P('ctx', 'tp')
- grad_w_down: float32 [4608, 1024], P('tp', 'ctx')
The draws below stay inside these ranges and needn't reach their ends.
Inputs may be any that keep to these rules, and one draw needn't show every extreme that they name: `positions`: strictly increasing along the sequence, starting at 0, steps of 1 to 3, the last equal to 16382. A permutation: stored rows j * 256 to (j + 1) * 256 - 1 hold span span_order[j] of the sequence.
All inputs are finite; a program needn't handle non-finite values.
Results may differ from the reference program's by a relative error of at most 0.03.
Values may be sent and summed in bfloat16 or wider, within the bound.
No kernel may reach another device: no remote copies, remote signals or barrier semaphores. Data moves between devices by JAX's collectives and lax.ppermute only.
A program may use at most 128 MiB of HBM per device.

```python
import math
import jax
import jax.numpy as jnp
from jax import lax

D = 1024
HQ = 16
HK = 8
HD = 64
FF = 4608
SEQ = 8192
SPANS = 32
SPAN = 256


def draw_positions(key, part):
    key = jax.random.fold_in(key, 11)
    offsets = jax.random.randint(key, (SEQ,), 0, 2)
    places = jnp.arange(SEQ, dtype=jnp.int32)
    offsets = jnp.where((places == 0) | (places == SEQ - 1), 0, offsets)
    return (2 * places - offsets).astype(jnp.int32)


def block_levels(rng, extent, shards, low, largest):
    def one(dim, shards_of):
        heights = jax.random.uniform(jax.random.fold_in(jax.random.fold_in(rng, 6), dim), (shards_of,), jnp.float32, low / len(shards), largest / len(shards))
        return jnp.repeat(jnp.exp(heights), extent[dim] // shards_of).reshape((-1,) + (1,) * (len(extent) - dim - 1))

    loudness = one(*shards[0])
    for cut in shards[1:]:
        loudness = loudness * one(*cut)
    return loudness


def noise(stream_key, shape, deviation, most, shards=(), kind=jnp.bfloat16):
    values = deviation * jax.random.normal(stream_key, shape, jnp.float32)
    if shards:
        values = values * block_levels(stream_key, shape, shards, -0.22, 0.18)
    return jnp.clip(values, -most, most).astype(kind)


def setup_inputs(seed: int = 0) -> dict:
    streams_of = jax.random.split(jax.random.key(seed), 16)
    return {
        "tokens": noise(streams_of[0], (SEQ, D), 1.0, 6.0, ((0, 128),)),
        "cotangent": noise(streams_of[1], (SEQ, D), 1.0, 6.0, ((0, 128),)),
        "positions": draw_positions(jax.random.fold_in(streams_of[15], 71), 0),
        "span_order": jax.random.permutation(streams_of[3], SPANS).astype(jnp.int32),
        "first_gain": jnp.clip(1.0 + 0.15 * jax.random.normal(streams_of[4], (D,), jnp.float32), 0.25, 1.75),
        "w_query": noise(streams_of[5], (D, HQ * HD), D ** -0.5, 0.1875, ((1, 8),)),
        "w_key": noise(streams_of[6], (D, HK * HD), D ** -0.5, 0.1875, ((1, 8),)),
        "w_value": noise(streams_of[7], (D, HK * HD), D ** -0.5, 0.1875, ((1, 8),)),
        "query_gain": jnp.clip(1.0 + 0.15 * jax.random.normal(streams_of[8], (HD,), jnp.float32), 0.25, 1.75),
        "key_gain": jnp.clip(1.0 + 0.15 * jax.random.normal(streams_of[9], (HD,), jnp.float32), 0.25, 1.75),
        "w_out": noise(streams_of[10], (HQ * HD, D), (HQ * HD // 64) ** -0.5, 1.5, ((0, 8),)),
        "second_gain": jnp.clip(1.0 + 0.15 * jax.random.normal(streams_of[11], (D,), jnp.float32), 0.25, 1.75),
        "w_gate": noise(streams_of[12], (D, FF), D ** -0.5, 0.1875, ((1, 8),)),
        "w_up": noise(streams_of[13], (D, FF), D ** -0.5, 0.1875, ((1, 8),)),
        "w_down": noise(streams_of[14], (FF, D), FF ** -0.5, 0.09375, ((0, 8),)),
    }


eps = 1e-05
theta = 1000000.0
highest = lax.Precision.HIGHEST

@jax.custom_vjp
def low(v):
    return lax.optimization_barrier(v.astype(jnp.bfloat16)).astype(jnp.float32)

@jax.custom_vjp
def low_back(v):
    return v

def low_keep(v):
    return (low(v), None)

def low_pass(kept, grad):
    return (grad,)

def back_keep(v):
    return (v, None)

def back_low(kept, grad):
    return (low(grad),)
low.defvjp(low_keep, low_pass)
low_back.defvjp(back_keep, back_low)

def rms_scaled(values, gain):
    scaled = values * lax.rsqrt(lax.optimization_barrier(jnp.mean(values * values, axis=-1, keepdims=True)) + eps)
    return scaled * gain

def rotate(values, cosine, sine):
    half = values.shape[-1] // 2
    first = values[..., :half]
    second = values[..., half:]
    return jnp.concatenate([first * cosine - second * sine, second * cosine + first * sine], axis=-1)

def angles(places, width):
    freqs = theta ** (-(jnp.arange(width // 2, dtype=jnp.float32) * 2.0 / width))
    turned = places.astype(jnp.float32)[:, None] * freqs[None, :]
    return (jnp.cos(turned), jnp.sin(turned))

def layer(tokens, first_gain, w_query, w_key, w_value, query_gain, key_gain, w_out, second_gain, w_gate, w_up, w_down, cosine, sine, order_index):
    normed = low(rms_scaled(tokens, first_gain))
    query_pre = low_back(jnp.dot(normed, w_query, precision=highest))
    key_pre = low_back(jnp.dot(normed, w_key, precision=highest))
    values = low(low_back(jnp.dot(normed, w_value, precision=highest)))
    group = HQ // HK
    queries = low(rotate(rms_scaled(query_pre.reshape(SEQ, HQ, HD), query_gain), cosine[:, None, :], sine[:, None, :]))
    keys = low(rotate(rms_scaled(key_pre.reshape(SEQ, HK, HD), key_gain), cosine[:, None, :], sine[:, None, :]))
    values = values.reshape(SEQ, HK, HD)
    block = math.gcd(SEQ, 512)
    count = SEQ // block
    query_blocks = queries.reshape(count, block, HK, group, HD)
    row_blocks = order_index.reshape(count, block)
    scale = 1.0 / math.sqrt(HD)

    def attend(pair):
        query_part, rows = pair
        scores = low_back(scale * jnp.einsum('qkgd,rkd->kgqr', query_part, keys, precision=highest))
        allowed = rows[:, None] >= order_index[None, :]
        scores = jnp.where(allowed[None, None], scores, -1e+30)
        weights = jax.nn.softmax(scores, axis=-1)
        return jnp.einsum('kgqr,rkd->qkgd', low(weights), values, precision=highest)
    attended = lax.map(jax.checkpoint(attend), (query_blocks, row_blocks))
    attended = low(low_back(attended.reshape(SEQ, HQ * HD)))
    resid = tokens + low_back(jnp.dot(attended, w_out, precision=highest))
    normed_two = low(rms_scaled(resid, second_gain))
    gate = low_back(jnp.dot(normed_two, w_gate, precision=highest))
    up = low_back(jnp.dot(normed_two, w_up, precision=highest))
    hidden = low(jax.nn.silu(gate) * up)
    return resid + low_back(jnp.dot(hidden, w_down, precision=highest))

def reference(tokens, cotangent, positions, span_order, first_gain, w_query, w_key, w_value, query_gain, key_gain, w_out, second_gain, w_gate, w_up, w_down):
    stored = jnp.arange(SEQ, dtype=jnp.int32)
    order_index = (span_order[stored // SPAN] * SPAN + stored % SPAN).astype(jnp.int32)
    cosine, sine = angles(positions[order_index], HD)
    params = (tokens, first_gain, w_query, w_key, w_value, query_gain, key_gain, w_out, second_gain, w_gate, w_up, w_down)
    params = tuple((p.astype(jnp.float32) for p in params))

    def forward(*inner):
        return layer(*inner, cosine, sine, order_index)
    result, pullback = jax.vjp(forward, *params)
    grads = pullback(cotangent.astype(jnp.float32))
    return (result.astype(jnp.bfloat16), grads[0].astype(jnp.bfloat16), grads[1], grads[2], grads[3], grads[4], grads[5], grads[6], grads[7], grads[8], grads[9], grads[10], grads[11])
```

```python
from functools import partial
import math

import jax
import jax.numpy as jnp
from jax import lax
from jax.experimental import pallas as pl
from jax.experimental.pallas import tpu as pltpu
from jax.sharding import PartitionSpec as P

eps = 1e-05
theta = 1000000.0
bf16 = jnp.bfloat16
f32 = jnp.float32
vmem_bytes = 56 * 1024 * 1024
log2e = math.log2(math.e)
HEAD = 64
LANES = 128


def dot(a, b):
    return jnp.dot(a, b, preferred_element_type=f32)


def dot_t(a, b):
    return lax.dot_general(a, b, (((1,), (1,)), ((), ())), preferred_element_type=f32)


def t_dot(a, b):
    return lax.dot_general(a, b, (((0,), (0,)), ((), ())), preferred_element_type=f32)


def call(kernel, out_shape, **more):
    return pl.pallas_call(
        kernel,
        out_shape=out_shape,
        compiler_params=pltpu.CompilerParams(vmem_limit_bytes=vmem_bytes),
        **more,
    )


def in_vmem(count):
    return [pl.BlockSpec(memory_space=pltpu.VMEM)] * count


in_smem = pl.BlockSpec(memory_space=pltpu.SMEM)


def exchange(x, axis, groups=None):
    return lax.all_to_all(x, axis, 0, 0, axis_index_groups=groups, tiled=True)


def spread(x, axis, count, groups=None):
    return exchange(jnp.broadcast_to(x[None], (count, *x.shape)), axis, groups)


def left_half(shape):
    return lax.broadcasted_iota(jnp.int32, shape, 1) < HEAD


def swap_quarters(v):
    lane = lax.broadcasted_iota(jnp.int32, v.shape, 1)
    return jnp.where(lane % HEAD < HEAD // 2, pltpu.roll(v, LANES - 32, 1), pltpu.roll(v, 32, 1))


def head_mean(v, left):
    first = jnp.sum(jnp.where(left, v, 0.0), axis=1, keepdims=True)
    second = jnp.sum(jnp.where(left, 0.0, v), axis=1, keepdims=True)
    return jnp.where(left, first, second) * (1.0 / HEAD)


def project_kernel(
    x_ref, gain_ref, w_ref, head_gain_ref, cos_ref, sin_ref,
    normed_ref, pre_ref, qx_ref, qz_ref, kv_ref,
):
    x = x_ref[...].astype(f32)
    scaled = x * lax.rsqrt(jnp.mean(x * x, axis=1, keepdims=True) + eps)
    normed = (scaled * gain_ref[...]).astype(bf16)
    normed_ref[...] = normed
    pre = dot(normed, w_ref[...])
    pre_ref[...] = pre
    cosine, sine = cos_ref[...], sin_ref[...]
    span = x.shape[0]
    left = left_half((span, LANES))

    def prepared(v, gain):
        v = v * lax.rsqrt(head_mean(v * v, left) + eps) * gain
        return v * cosine + swap_quarters(v) * sine

    query = prepared(pre[:, :LANES], head_gain_ref[0:1, :])
    pair = pre[:, LANES:]
    key = prepared(pair, head_gain_ref[1:2, :])
    kv_ref[...] = jnp.where(left, key, pair).astype(bf16)
    for head in range(2):
        own = query if head == 0 else pltpu.roll(query, HEAD, 1)
        own = jnp.where(left, own, 0.0)
        rows = pl.ds(head * span, span)
        qx_ref[rows, :] = (own * (log2e / math.sqrt(HEAD))).astype(bf16)
        qz_ref[rows, :] = (own.astype(bf16).astype(f32) * (1.0 / math.sqrt(HEAD))).astype(bf16)


def earlier_spans(order_ref, list_ref, rank, core, blocks):
    def look(block, count):
        list_ref[count] = block
        slot = ((block // 2) * 2 + core) * 2 + block % 2
        return count + (order_ref[slot] < rank).astype(jnp.int32)

    return lax.fori_loop(0, blocks, look, jnp.int32(0))


def block_rows(index, span):
    return pl.ds(pl.multiple_of(index * span, span), span)


def in_groups(count, size, body):
    whole = count // size

    def some(step, carry):
        body([step * size + k for k in range(size)])
        return carry

    lax.fori_loop(0, whole, some, 0)

    def one(step, carry):
        body([step])
        return carry

    lax.fori_loop(whole * size, count, one, 0)


def attend_kernel(last, order_ref, qx_ref, kv_ref, *refs):
    if last:
        start_ref, out_ref, attended_ref, list_ref, acc_ref = refs
    else:
        acc_ref, list_ref = refs
    me = lax.axis_index("ctx")
    core = me % 2
    side = 1 - core if last else core
    span = qx_ref.shape[0] // 4
    blocks = kv_ref.shape[0] // span
    left = left_half((span, LANES))
    one = jnp.ones((span, LANES), bf16)
    for slot in range(2):
        rows = pl.ds(slot * 2 * span, 2 * span)
        count = earlier_spans(order_ref, list_ref, order_ref[me * 2 + slot], side, blocks)

        def product(index, mask=None):
            pair = kv_ref[block_rows(index, span), :]
            weights = jnp.exp2(dot_t(qx_ref[rows, :], pair))
            if mask is not None:
                weights = jnp.where(mask, weights, 0.0)
            return dot(weights.astype(bf16), jnp.where(left, one, pair))

        if last:
            acc_ref[rows, :] = start_ref[rows, :]
        else:
            row = lax.broadcasted_iota(jnp.int32, (2 * span, span), 0) % span
            col = lax.broadcasted_iota(jnp.int32, (2 * span, span), 1)
            acc_ref[rows, :] = product((me // 2) * 2 + slot, row >= col)

        def add(steps):
            acc_ref[rows, :] += sum(product(list_ref[step]) for step in steps)

        in_groups(count, 4, add)
        if last:
            for head in range(2):
                part = pl.ds((slot * 2 + head) * span, span)
                acc = acc_ref[part, :]
                turned = pltpu.roll(acc, HEAD, 1)
                out = jnp.where(left, jnp.log2(acc), acc / jnp.where(left, 1.0, turned))
                out_ref[part, :] = out
                if head == 0:
                    first = pltpu.roll(out, HEAD, 1)
                else:
                    attended_ref[pl.ds(slot * span, span), :] = jnp.where(left, first, out).astype(bf16)


def pull_kernel(last, order_ref, kv_ref, qz_ref, *refs):
    if last:
        qb_ref, dx_ref, dz_ref, start_ref, dkv_ref, dq_ref, list_ref = refs
        dq_ref[...] = start_ref[...]
    else:
        qx_ref, out_ref, base_ref, recv_ref, dkv_ref, dq_ref, qb_ref, dx_ref, dz_ref, list_ref = refs
        dq_ref[...] = jnp.zeros_like(dq_ref)
    dkv_ref[...] = jnp.zeros_like(dkv_ref)
    me = lax.axis_index("ctx")
    core = me % 2
    side = core if last else 1 - core
    span = qz_ref.shape[0] // 4
    blocks = kv_ref.shape[0] // span
    left = left_half((span, LANES))
    lane = lax.broadcasted_iota(jnp.int32, (span, LANES), 1)
    one = jnp.ones((span, LANES), bf16)
    if not last:
        for slot in range(2):
            rows = pl.ds(slot * span, span)
            mixed = base_ref[rows, :]
            for peer in range(recv_ref.shape[0]):
                mixed = mixed + recv_ref[peer, rows, :].astype(f32)
            mixed = mixed.astype(bf16).astype(f32)
            for head in range(2):
                part = pl.ds((slot * 2 + head) * span, span)
                own = jnp.where(left, 0.0, pltpu.roll(mixed, HEAD, 1) if head == 0 else mixed)
                dz_ref[part, :] = own.astype(bf16)
                out = out_ref[part, :]
                delta = jnp.sum(own * out, axis=1, keepdims=True)
                high = delta.astype(bf16).astype(f32)
                low = (delta - high).astype(bf16).astype(f32)
                own = jnp.where(lane == 0, -high, jnp.where(lane == 1, -low, own))
                dx_ref[part, :] = own.astype(bf16)
                total = pltpu.roll(out, HEAD, 1)
                high = total.astype(bf16).astype(f32)
                middle = (total - high).astype(bf16).astype(f32)
                low = total - high - middle
                query = qx_ref[part, :].astype(f32)
                query = jnp.where(lane == HEAD, -high, query)
                query = jnp.where(lane == HEAD + 1, -middle, query)
                query = jnp.where(lane == HEAD + 2, -low, query)
                qb_ref[part, :] = query.astype(bf16)
    for slot in range(2):
        rows = pl.ds(slot * 2 * span, 2 * span)
        count = earlier_spans(order_ref, list_ref, order_ref[me * 2 + slot], side, blocks)

        def product(index, mask=None):
            part = block_rows(index, span)
            pair = kv_ref[part, :]
            weights = jnp.exp2(dot_t(jnp.where(left, pair, one), qb_ref[rows, :]))
            if mask is not None:
                weights = jnp.where(mask, weights, 0.0)
            pulled = dot_t(jnp.where(left, one, pair), dx_ref[rows, :])
            score = (weights * pulled).astype(bf16)
            dkv_ref[part, :] += dot(score, qz_ref[rows, :]) + dot(weights.astype(bf16), dz_ref[rows, :])
            return t_dot(score, pair)

        def add(steps):
            dq_ref[rows, :] += sum(product(list_ref[step]) for step in steps)

        if last:
            row = lax.broadcasted_iota(jnp.int32, (span, 2 * span), 0)
            col = lax.broadcasted_iota(jnp.int32, (span, 2 * span), 1) % span
            dq_ref[rows, :] += product((me // 2) * 2 + slot, col >= row)
        in_groups(count, 2, add)


def back_kernel(
    dq_ref, recv_ref, pre_ref, head_gain_ref, cos_ref, sin_ref, pre_grad_ref, head_sums_ref
):
    span = cos_ref.shape[0] // 2
    left = left_half((span, LANES))

    def pulled(grad, pre, gain, cosine, sine):
        turned = grad * cosine - swap_quarters(grad) * sine
        factor = lax.rsqrt(head_mean(pre * pre, left) + eps)
        unit = pre * factor
        sums = jnp.sum(turned * unit, axis=0, keepdims=True)
        scaled = turned * gain
        return (scaled - unit * head_mean(scaled * unit, left)) * factor, sums

    totals = [0.0, 0.0]
    for slot in range(2):
        rows = pl.ds(slot * span, span)
        cosine, sine = cos_ref[rows, :], sin_ref[rows, :]
        first = dq_ref[pl.ds(slot * 2 * span, span), :]
        second = dq_ref[pl.ds((slot * 2 + 1) * span, span), :]
        grad = jnp.where(left, first, pltpu.roll(second, HEAD, 1)) * (1.0 / math.sqrt(HEAD))
        pair = recv_ref[0, rows, :].astype(f32)
        for peer in range(1, recv_ref.shape[0]):
            pair = pair + recv_ref[peer, rows, :].astype(f32)
        query, sums = pulled(
            grad, pre_ref[rows, :LANES], head_gain_ref[0:1, :], cosine, sine
        )
        totals[0] = totals[0] + sums
        key, sums = pulled(
            jnp.where(left, pair, 0.0), pre_ref[rows, LANES:], head_gain_ref[1:2, :], cosine, sine
        )
        totals[1] = totals[1] + sums
        pre_grad_ref[rows, :LANES] = query.astype(bf16)
        pre_grad_ref[rows, LANES:] = jnp.where(left, key, pair).astype(bf16)
    folded = totals[0] + pltpu.roll(totals[0], HEAD, 1)
    head_sums_ref[...] = jnp.where(left_half((1, LANES)), folded, pltpu.roll(totals[1], HEAD, 1))


def turning(positions, span_order, me, span):
    table = positions.reshape(-1, span)
    own = [lax.dynamic_index_in_dim(table, span_order[me * 2 + k], 0, False) for k in range(2)]
    places = jnp.concatenate(own).astype(f32)
    freqs = theta ** (-(jnp.arange(HEAD // 2, dtype=f32) * 2.0 / HEAD))
    turned = places[:, None] * freqs[None, :]
    cosine, sine = jnp.cos(turned), jnp.sin(turned)
    return (
        jnp.concatenate([cosine] * 4, axis=1),
        jnp.concatenate([-sine, sine, -sine, sine], axis=1),
    )


def per_device(
    tokens, cotangent, positions, span_order, first_gain, w_query, w_key, w_value,
    query_gain, key_gain, w_out, second_gain, w_gate, w_up, w_down,
):
    ctx_count = lax.axis_size("ctx")
    tp_count = lax.axis_size("tp")
    me = lax.axis_index("ctx")
    mine = lax.axis_index("tp")
    part, width = tokens.shape
    local = part * tp_count
    span = local // 2
    half = ctx_count // 2
    heads = w_out.shape[0]
    hidden_width = w_gate.shape[1]
    same_core = [[2 * k + core for k in range(half)] for core in range(2)]
    other_core = [(k, k ^ 1) for k in range(ctx_count)]
    shape = jax.ShapeDtypeStruct

    x_all = spread(tokens, "tp", tp_count).reshape(local, width)
    side = lax.all_gather(jnp.concatenate([cotangent, w_out], axis=0), "tp", axis=0, tiled=False)
    dy_all = side[:, :part].reshape(local, width)
    w_out_all = side[:, part:]
    w_qkv = jnp.concatenate([w_query, w_key, w_value], axis=1)
    w_qkv_all = lax.all_gather(w_qkv, "tp", axis=0, tiled=False)
    cosine, sine = turning(positions, span_order, me, span)
    head_gain = jnp.stack(
        [jnp.concatenate([query_gain, query_gain]), jnp.concatenate([key_gain, jnp.ones_like(key_gain)])]
    )

    by_span = lambda rows, cols: pl.BlockSpec((rows, cols), lambda k: (k, 0))
    whole = lambda a: pl.BlockSpec(a.shape, lambda k: (0, 0))
    gain_row = first_gain.reshape(1, width)
    normed, pre, qx, qz, kv = call(
        project_kernel,
        (
            shape((local, width), bf16),
            shape((local, 2 * LANES), f32),
            shape((2 * local, LANES), bf16),
            shape((2 * local, LANES), bf16),
            shape((local, LANES), bf16),
        ),
        grid=(2,),
        in_specs=[
            by_span(span, width), whole(gain_row), whole(w_qkv), whole(head_gain),
            by_span(span, LANES), by_span(span, LANES),
        ],
        out_specs=(
            by_span(span, width), by_span(span, 2 * LANES), by_span(2 * span, LANES),
            by_span(2 * span, LANES), by_span(span, LANES),
        ),
        name="project",
    )(x_all, gain_row, w_qkv, head_gain, cosine, sine)

    kv_own = spread(kv, "ctx", half, same_core).reshape(half * local, LANES)
    kv_other = lax.ppermute(kv_own, "ctx", other_core)
    acc = call(
        partial(attend_kernel, False),
        shape((2 * local, LANES), f32),
        in_specs=[in_smem, *in_vmem(2)],
        out_specs=pl.BlockSpec(memory_space=pltpu.VMEM),
        scratch_shapes=[pltpu.SMEM((ctx_count + 1,), jnp.int32)],
        cost_estimate=pl.CostEstimate(flops=4 * 10**9, bytes_accessed=2**21, transcendentals=2**22),
        name="attend_own",
    )(span_order, qx, kv_own)
    out, attended = call(
        partial(attend_kernel, True),
        (shape((2 * local, LANES), f32), shape((local, LANES), bf16)),
        in_specs=[in_smem, *in_vmem(3)],
        out_specs=tuple(in_vmem(2)),
        scratch_shapes=[pltpu.SMEM((ctx_count + 1,), jnp.int32), pltpu.VMEM((2 * local, LANES), f32)],
        cost_estimate=pl.CostEstimate(flops=4 * 10**9, bytes_accessed=2**21, transcendentals=2**22),
        name="attend_other",
    )(span_order, qx, kv_other, acc)

    attended_all = spread(attended, "tp", tp_count)
    resid = x_all.astype(f32) + jnp.einsum(
        "tsd,tdm->sm", attended_all, w_out_all, preferred_element_type=f32
    )
    factor = lax.rsqrt(jnp.mean(resid * resid, axis=1, keepdims=True) + eps)
    unit = resid * factor
    normed_two = (unit * second_gain).astype(bf16)
    gate = dot(normed_two, w_gate)
    up = dot(normed_two, w_up)
    hidden_grad = dot_t(dy_all, w_down)
    sigma = jax.nn.sigmoid(gate)
    swish = gate * sigma
    hidden = (swish * up).astype(bf16)
    gate_grad = (hidden_grad * up * sigma * (1.0 + gate * (1.0 - sigma))).astype(bf16)
    up_grad = (hidden_grad * swish).astype(bf16)
    second_grad = dot_t(gate_grad, w_gate) + dot_t(up_grad, w_up)
    scaled = second_grad * second_gain
    resid_part = ((scaled - unit * jnp.mean(scaled * unit, axis=1, keepdims=True)) * factor).astype(bf16)
    second_sum = jnp.sum(second_grad * unit, axis=0)
    mixed_part = jnp.einsum("sm,tdm->tsd", resid_part, w_out_all, preferred_element_type=f32)
    mixed_recv = exchange(mixed_part.astype(bf16), "tp")
    mixed_base = dot_t(dy_all, w_out)

    down = dot(hidden, w_down).astype(bf16)
    rows_recv = exchange(
        jnp.concatenate([resid_part, down], axis=1).reshape(tp_count, part, 2 * width), "tp"
    )
    rows_sum = jnp.sum(rows_recv.astype(f32), axis=0)
    own_resid = lax.dynamic_slice_in_dim(resid, mine * part, part, 0)
    block_out = (own_resid + rows_sum[:, width:]).astype(bf16)
    resid_grad = cotangent.astype(f32) + rows_sum[:, :width]
    resid_grad_all = spread(resid_grad.astype(bf16), "tp", tp_count).reshape(local, width)
    grad_out = t_dot(resid_grad_all, attended)

    feed = jnp.concatenate(
        [t_dot(normed_two, gate_grad), t_dot(normed_two, up_grad), t_dot(dy_all, hidden)], axis=1
    ).astype(bf16)
    feed = lax.psum_scatter(feed, "ctx", scatter_dimension=0, tiled=True).astype(f32)
    grad_gate = feed[:, :hidden_width]
    grad_up = feed[:, hidden_width : 2 * hidden_width]
    grad_down = feed[:, 2 * hidden_width :].T

    dkv_shape = shape((half * local, LANES), f32)
    dq_shape = shape((2 * local, LANES), f32)
    q_shape = shape((2 * local, LANES), bf16)
    dkv_other, dq_other, qb, dx, dz = call(
        partial(pull_kernel, False),
        (dkv_shape, dq_shape, q_shape, q_shape, q_shape),
        in_specs=[in_smem, *in_vmem(6)],
        out_specs=tuple(in_vmem(5)),
        scratch_shapes=[pltpu.SMEM((ctx_count + 1,), jnp.int32)],
        cost_estimate=pl.CostEstimate(flops=10 * 10**9, bytes_accessed=2**22, transcendentals=2**22),
        name="pull_other",
    )(span_order, kv_other, qz, qx, out, mixed_base, mixed_recv)
    dkv_moved = lax.ppermute(dkv_other.astype(bf16), "ctx", other_core)
    dkv_own, dq = call(
        partial(pull_kernel, True),
        (dkv_shape, dq_shape),
        in_specs=[in_smem, *in_vmem(6)],
        out_specs=tuple(in_vmem(2)),
        scratch_shapes=[pltpu.SMEM((ctx_count + 1,), jnp.int32)],
        cost_estimate=pl.CostEstimate(flops=10 * 10**9, bytes_accessed=2**22, transcendentals=2**22),
        name="pull_own",
    )(span_order, kv_own, qz, qb, dx, dz, dq_other)
    dkv = (dkv_own + dkv_moved.astype(f32)).astype(bf16).reshape(half, local, LANES)
    dkv_recv = exchange(dkv, "ctx", same_core)

    pre_grad, head_sums = call(
        back_kernel,
        (shape((local, 2 * LANES), bf16), shape((1, LANES), f32)),
        in_specs=in_vmem(6),
        out_specs=tuple(in_vmem(2)),
        name="back",
    )(dq, dkv_recv, pre, head_gain, cosine, sine)
    grad_qkv = t_dot(normed, pre_grad)
    first_sum = jnp.sum(grad_qkv * w_qkv.astype(f32), axis=1) / first_gain
    sums = jnp.concatenate([first_sum, second_sum, head_sums[0], jnp.zeros((LANES,), f32)])
    extra = 16
    cols = 2 * LANES

    def with_sums(blocks, sums, count):
        rows = jnp.pad(sums.astype(bf16).reshape(-1, cols), ((0, extra - sums.shape[0] // cols), (0, 0)))
        if blocks.shape[2] > cols:
            rows = jnp.pad(rows, ((0, 0), (0, blocks.shape[2] - cols)))
        return jnp.concatenate([blocks, jnp.broadcast_to(rows[None], (count, extra, rows.shape[1]))], axis=1)

    tp_recv = exchange(with_sums(pre_grad.reshape(tp_count, part, cols), sums, tp_count), "tp")
    sums = jnp.sum(tp_recv[:, part:].astype(f32), axis=0)[: sums.shape[0] // cols].reshape(-1)
    grad_blocks = jnp.concatenate([grad_qkv, grad_out], axis=1).astype(bf16)
    grad_blocks = grad_blocks.reshape(ctx_count, width // ctx_count, cols + LANES)
    ctx_recv = jnp.sum(exchange(with_sums(grad_blocks, sums, ctx_count), "ctx").astype(f32), axis=0)
    own_width = width // ctx_count
    sums = ctx_recv[own_width:, :cols][: sums.shape[0] // cols].reshape(-1)
    grads = ctx_recv[:own_width]

    normed_grad = jnp.einsum(
        "tsc,tdc->sd", tp_recv[:, :part], w_qkv_all, preferred_element_type=f32
    )
    x = tokens.astype(f32)
    factor = lax.rsqrt(jnp.mean(x * x, axis=1, keepdims=True) + eps)
    unit = x * factor
    scaled = normed_grad * first_gain
    tokens_part = (scaled - unit * jnp.mean(scaled * unit, axis=1, keepdims=True)) * factor
    grad_tokens = (resid_grad + tokens_part).astype(bf16)
    return (
        block_out,
        grad_tokens,
        sums[:width],
        grads[:, :LANES],
        grads[:, LANES : LANES + HEAD],
        grads[:, LANES + HEAD : cols],
        sums[2 * width : 2 * width + HEAD],
        sums[2 * width + HEAD : 2 * width + 2 * HEAD],
        grads[:, cols:].T,
        sums[width : 2 * width],
        grad_gate,
        grad_up,
        grad_down,
    )


def solution(mesh):
    return jax.shard_map(
        per_device,
        mesh=mesh,
        in_specs=(
            P(("ctx", "tp"), None),
            P(("ctx", "tp"), None),
            P(),
            P(),
            P(),
            P(None, "tp"),
            P(None, "tp"),
            P(None, "tp"),
            P(),
            P(),
            P("tp", None),
            P(),
            P(None, "tp"),
            P(None, "tp"),
            P("tp", None),
        ),
        out_specs=(
            P(("ctx", "tp"), None),
            P(("ctx", "tp"), None),
            P(),
            P("ctx", "tp"),
            P("ctx", "tp"),
            P("ctx", "tp"),
            P(),
            P(),
            P("tp", "ctx"),
            P(),
            P("ctx", "tp"),
            P("ctx", "tp"),
            P("tp", "ctx"),
        ),
        check_vma=False,
    )
```

```python
from functools import partial
import math

import jax
import jax.numpy as jnp
from jax import lax
from jax.experimental import pallas as pl
from jax.experimental.pallas import tpu as pltpu
from jax.sharding import PartitionSpec as P

eps = 1e-05
theta = 1000000.0
bf16 = jnp.bfloat16
f32 = jnp.float32
vmem_bytes = 56 * 1024 * 1024
log2e = math.log2(math.e)
HEAD = 64
LANES = 128


def dot(a, b):
    return jnp.dot(a, b, preferred_element_type=f32)


def dot_t(a, b):
    return lax.dot_general(a, b, (((1,), (1,)), ((), ())), preferred_element_type=f32)


def t_dot(a, b):
    return lax.dot_general(a, b, (((0,), (0,)), ((), ())), preferred_element_type=f32)


def call(kernel, out_shape, **more):
    return pl.pallas_call(
        kernel,
        out_shape=out_shape,
        compiler_params=pltpu.CompilerParams(vmem_limit_bytes=vmem_bytes),
        **more,
    )


def in_vmem(count):
    return [pl.BlockSpec(memory_space=pltpu.VMEM)] * count


in_smem = pl.BlockSpec(memory_space=pltpu.SMEM)


def exchange(x, axis, groups=None):
    return lax.all_to_all(x, axis, 0, 0, axis_index_groups=groups, tiled=True)


def spread(x, axis, count, groups=None):
    return exchange(jnp.broadcast_to(x[None], (count, *x.shape)), axis, groups)


def left_half(shape):
    return lax.broadcasted_iota(jnp.int32, shape, 1) < HEAD


def swap_quarters(v):
    lane = lax.broadcasted_iota(jnp.int32, v.shape, 1)
    return jnp.where(lane % HEAD < HEAD // 2, pltpu.roll(v, LANES - 32, 1), pltpu.roll(v, 32, 1))


def head_mean(v, left):
    first = jnp.sum(jnp.where(left, v, 0.0), axis=1, keepdims=True)
    second = jnp.sum(jnp.where(left, 0.0, v), axis=1, keepdims=True)
    return jnp.where(left, first, second) * (1.0 / HEAD)


def project_kernel(
    x_ref, gain_ref, w_ref, head_gain_ref, cos_ref, sin_ref, normed_ref, pre_ref, query_ref, kv_ref
):
    x = x_ref[...].astype(f32)
    scaled = x * lax.rsqrt(jnp.mean(x * x, axis=1, keepdims=True) + eps)
    normed = (scaled * gain_ref[...]).astype(bf16)
    normed_ref[...] = normed
    pre = dot(normed, w_ref[...])
    pre_ref[...] = pre
    cosine, sine = cos_ref[...], sin_ref[...]
    left = left_half((x.shape[0], LANES))

    def prepared(v, gain):
        v = v * lax.rsqrt(head_mean(v * v, left) + eps) * gain
        return v * cosine + swap_quarters(v) * sine

    query = prepared(pre[:, :LANES], head_gain_ref[0:1, :])
    query_ref[...] = (query * (log2e / math.sqrt(HEAD))).astype(bf16)
    pair = pre[:, LANES:]
    key = prepared(pair, head_gain_ref[1:2, :])
    both = jnp.where(left, key, pair).astype(bf16)
    for peer in range(kv_ref.shape[0]):
        kv_ref[peer] = both


def earlier_spans(order_ref, list_ref, rank, core, blocks):
    def look(block, count):
        list_ref[count] = block
        slot = ((block // 2) * 2 + core) * 2 + block % 2
        return count + (order_ref[slot] < rank).astype(jnp.int32)

    return lax.fori_loop(0, blocks, look, jnp.int32(0))


def block_rows(index, span):
    return pl.ds(pl.multiple_of(index * span, span), span)


def in_groups(count, size, body):
    whole = count // size

    def some(step, carry):
        body([step * size + k for k in range(size)])
        return carry

    lax.fori_loop(0, whole, some, 0)

    def one(step, carry):
        body([step])
        return carry

    lax.fori_loop(whole * size, count, one, 0)


def pieces(v, count):
    parts = []
    for _ in range(count):
        part = v.astype(bf16).astype(f32)
        parts.append(part)
        v = v - part
    return parts


def attend_kernel(order_ref, own_ref, other_ref, kv_ref, acc_ref, sent_ref, list_ref, qx_ref, part_ref):
    me = lax.axis_index("ctx")
    core = me % 2
    span = own_ref.shape[0] // 2
    blocks = kv_ref.shape[0] // span
    left = left_half((span, LANES))
    lane = lax.broadcasted_iota(jnp.int32, (span, LANES), 1)
    one = jnp.ones((span, LANES), bf16)
    for source in range(2):
        for slot in range(2):
            query = (own_ref, other_ref)[source][pl.ds(slot * span, span), :].astype(f32)
            for head in range(2):
                own = query if head == 0 else pltpu.roll(query, HEAD, 1)
                qx_ref[pl.ds(head * span, span), :] = jnp.where(left, own, 0.0).astype(bf16)
            rank = order_ref[(me + source * (1 - 2 * core)) * 2 + slot]
            count = earlier_spans(order_ref, list_ref, rank, core, blocks)
            rows = pl.ds(slot * 2 * span, 2 * span)

            def product(index, mask=None):
                pair = kv_ref[block_rows(index, span), :]
                weights = jnp.exp2(dot_t(qx_ref[...], pair))
                if mask is not None:
                    weights = jnp.where(mask, weights, 0.0)
                return dot(weights.astype(bf16), jnp.where(left, one, pair))

            target = acc_ref if source == 0 else part_ref
            if source == 0:
                row = lax.broadcasted_iota(jnp.int32, (2 * span, span), 0) % span
                col = lax.broadcasted_iota(jnp.int32, (2 * span, span), 1)
                target[rows, :] = product((me // 2) * 2 + slot, row >= col)
            else:
                target[rows, :] = jnp.zeros((2 * span, LANES), f32)

            def add(steps):
                target[rows, :] += sum(product(list_ref[step]) for step in steps)

            in_groups(count, 4, add)
            if source == 1:
                for head in range(2):
                    part = pl.ds((slot * 2 + head) * span, span)
                    acc = target[part, :]
                    high, middle, low = pieces(acc, 3)
                    packed = jnp.where(lane == 0, high, jnp.where(lane == 1, middle, low))
                    packed = jnp.where(lane < 3, packed, jnp.where(left, 0.0, acc))
                    sent_ref[part, :] = packed.astype(bf16)


def finish_kernel(acc_ref, recv_ref, query_ref, out_ref, attended_ref, qb_ref):
    span = query_ref.shape[0] // 2
    left = left_half((span, LANES))
    lane = lax.broadcasted_iota(jnp.int32, (span, LANES), 1)
    for slot in range(2):
        rows = pl.ds(slot * span, span)
        query = query_ref[rows, :].astype(f32)
        outs = []
        for head in range(2):
            part = pl.ds((slot * 2 + head) * span, span)
            recv = recv_ref[part, :].astype(f32)
            acc = acc_ref[part, :]
            total = jnp.sum(jnp.where(left, recv, 0.0), axis=1, keepdims=True)
            total = total + jnp.where(left, acc, pltpu.roll(acc, HEAD, 1))
            logs = jnp.log2(total)
            out = jnp.where(left, logs, (acc + recv) / total)
            out_ref[part, :] = out
            outs.append(out)
            high, middle, low = pieces(logs, 3)
            own = jnp.where(left, query if head == 0 else pltpu.roll(query, HEAD, 1), 0.0)
            own = jnp.where(lane == HEAD, -high, own)
            own = jnp.where(lane == HEAD + 1, -middle, own)
            own = jnp.where(lane == HEAD + 2, -low, own)
            qb_ref[part, :] = own.astype(bf16)
        both = jnp.where(left, pltpu.roll(outs[0], HEAD, 1), outs[1]).astype(bf16)
        for peer in range(attended_ref.shape[0]):
            attended_ref[peer, rows, :] = both


def prepare_kernel(base_ref, recv_ref, out_ref, dx_ref):
    span = base_ref.shape[0] // 2
    left = left_half((span, LANES))
    lane = lax.broadcasted_iota(jnp.int32, (span, LANES), 1)
    for slot in range(2):
        rows = pl.ds(slot * span, span)
        mixed = base_ref[rows, :]
        for peer in range(recv_ref.shape[0]):
            mixed = mixed + recv_ref[peer, rows, :].astype(f32)
        mixed = mixed.astype(bf16).astype(f32)
        for head in range(2):
            part = pl.ds((slot * 2 + head) * span, span)
            own = jnp.where(left, 0.0, pltpu.roll(mixed, HEAD, 1) if head == 0 else mixed)
            delta = jnp.sum(own * out_ref[part, :], axis=1, keepdims=True)
            high, low = pieces(delta, 2)
            own = jnp.where(lane == 0, -high, jnp.where(lane == 1, -low, own))
            dx_ref[part, :] = own.astype(bf16)


def pull_kernel(last, order_ref, kv_ref, qb_ref, dx_ref, *refs):
    if last:
        start_ref, out_ref, dq_out_ref, list_ref, qz_ref, dz_ref, dkv_ref, dq_ref = refs
        dkv_ref[...] = start_ref[...]
    else:
        dkv_ref, dq_out_ref, list_ref, qz_ref, dz_ref, dq_ref = refs
        dkv_ref[...] = jnp.zeros_like(dkv_ref)
    me = lax.axis_index("ctx")
    core = me % 2
    whose = me + 1 - 2 * core if last else me
    span = qb_ref.shape[0] // 4
    blocks = kv_ref.shape[0] // span
    left = left_half((span, LANES))
    one = jnp.ones((span, LANES), bf16)
    zero = jnp.zeros((2 * span, LANES), bf16)
    wide_left = left_half((2 * span, LANES))
    for slot in range(2):
        rows = pl.ds(slot * 2 * span, 2 * span)
        qz_ref[...] = jnp.where(wide_left, qb_ref[rows, :], zero)
        dz_ref[...] = jnp.where(wide_left, zero, dx_ref[rows, :])
        count = earlier_spans(order_ref, list_ref, order_ref[whose * 2 + slot], core, blocks)

        def product(index, mask=None):
            part = block_rows(index, span)
            pair = kv_ref[part, :]
            weights = jnp.exp2(dot_t(jnp.where(left, pair, one), qb_ref[rows, :]))
            if mask is not None:
                weights = jnp.where(mask, weights, 0.0)
            pulled = dot_t(jnp.where(left, one, pair), dx_ref[rows, :])
            score = (weights * pulled).astype(bf16)
            dkv_ref[part, :] += dot(score, qz_ref[...]) + dot(weights.astype(bf16), dz_ref[...])
            return t_dot(score, pair)

        if last:
            dq_ref[...] = jnp.zeros_like(dq_ref)
        else:
            row = lax.broadcasted_iota(jnp.int32, (span, 2 * span), 0)
            col = lax.broadcasted_iota(jnp.int32, (span, 2 * span), 1) % span
            dq_ref[...] = product((me // 2) * 2 + slot, col >= row)

        def add(steps):
            dq_ref[...] += sum(product(list_ref[step]) for step in steps)

        in_groups(count, 2, add)
        both = jnp.where(left, dq_ref[:span, :], pltpu.roll(dq_ref[span:, :], HEAD, 1))
        dq_out_ref[pl.ds(slot * span, span), :] = both.astype(dq_out_ref.dtype)
    if last:
        factor = jnp.where(left_half((1, LANES)), 1.0 / log2e, 1.0)
        out_ref[...] = (dkv_ref[...] * factor).astype(bf16)


def rows_kernel(recv_ref, cotangent_ref, resid_ref, grad_ref, block_ref):
    width = resid_ref.shape[1]
    total = recv_ref[0].astype(f32)
    for peer in range(1, recv_ref.shape[0]):
        total = total + recv_ref[peer].astype(f32)
    grad_ref[...] = cotangent_ref[...].astype(f32) + total[:, :width]
    block_ref[...] = (resid_ref[...] + total[:, width:]).astype(bf16)


def as_rows(v):
    return jnp.concatenate([v[:, k : k + LANES] for k in range(0, v.shape[1], LANES)], axis=0)


def back_kernel(
    dq_ref, dq_recv_ref, recv_ref, pre_ref, head_gain_ref, cos_ref, sin_ref, w_ref, normed_ref,
    gain_ref, second_ref, grad_ref, pre_grad_ref, sent_ref,
):
    span = cos_ref.shape[0] // 2
    peers, _, width = sent_ref.shape
    part = 2 * span // peers
    left = left_half((span, LANES))

    def pulled(grad, pre, gain, cosine, sine):
        turned = grad * cosine - swap_quarters(grad) * sine
        factor = lax.rsqrt(head_mean(pre * pre, left) + eps)
        unit = pre * factor
        sums = jnp.sum(turned * unit, axis=0, keepdims=True)
        scaled = turned * gain
        return (scaled - unit * head_mean(scaled * unit, left)) * factor, sums

    totals = [0.0, 0.0, 0.0]
    for slot in range(2):
        rows = pl.ds(slot * span, span)
        cosine, sine = cos_ref[rows, :], sin_ref[rows, :]
        grad = (dq_ref[rows, :] + dq_recv_ref[rows, :].astype(f32)) * (1.0 / math.sqrt(HEAD))
        pair = recv_ref[0, rows, :].astype(f32)
        for peer in range(1, recv_ref.shape[0]):
            pair = pair + recv_ref[peer, rows, :].astype(f32)
        query, sums = pulled(grad, pre_ref[rows, :LANES], head_gain_ref[0:1, :], cosine, sine)
        totals[0] = totals[0] + sums
        key, sums = pulled(
            jnp.where(left, pair, 0.0), pre_ref[rows, LANES:], head_gain_ref[1:2, :], cosine, sine
        )
        totals[1] = totals[1] + sums
        pre_grad_ref[rows, :LANES] = query.astype(bf16)
        pre_grad_ref[rows, LANES:] = jnp.where(left, key, pair).astype(bf16)
        normed_part = dot_t(pre_grad_ref[rows, :], w_ref[...])
        totals[2] = totals[2] + jnp.sum(
            normed_part * normed_ref[rows, :].astype(f32), axis=0, keepdims=True
        )
        sent = normed_part.astype(bf16).reshape(peers // 2, part, width)
        sent_ref[slot * (peers // 2) : (slot + 1) * (peers // 2), :part, :] = sent
    folded = totals[0] + pltpu.roll(totals[0], HEAD, 1)
    heads = jnp.where(left_half((1, LANES)), folded, pltpu.roll(totals[1], HEAD, 1))
    sums = jnp.concatenate(
        [as_rows(totals[2] / gain_ref[...]), as_rows(second_ref[...]), jnp.broadcast_to(heads, (8, LANES))],
        axis=1,
    )
    sums = jnp.concatenate([sums, jnp.zeros_like(sums)], axis=0).astype(bf16)
    for peer in range(peers):
        sent_ref[peer, part : 2 * part, :] = grad_ref[...].astype(bf16)
        sent_ref[peer, 2 * part :, : 3 * LANES] = sums
        sent_ref[peer, 2 * part :, 3 * LANES :] = jnp.zeros((16, width - 3 * LANES), bf16)


def tokens_kernel(
    recv_ref, tokens_ref, gain_ref, resid_grad_ref, attended_ref, grad_ref, own_ref, other_ref,
    flat_ref,
):
    part = tokens_ref.shape[0]
    rows = own_ref.shape[0] - 16
    total = recv_ref[0, :part].astype(f32)
    sums = recv_ref[0, 2 * part :, : 3 * LANES].astype(f32)
    for peer in range(1, recv_ref.shape[0]):
        total = total + recv_ref[peer, :part].astype(f32)
        sums = sums + recv_ref[peer, 2 * part :, : 3 * LANES].astype(f32)
    for peer in range(recv_ref.shape[0]):
        flat_ref[peer * part : (peer + 1) * part, :] = recv_ref[peer, part : 2 * part]
    by_core(
        own_ref, other_ref, slice(0, rows), slice(0, LANES), t_dot(flat_ref[...], attended_ref[...])
    )
    for target in (own_ref, other_ref):
        target[:rows, LANES:] = jnp.zeros((rows, 2 * LANES), bf16)
        target[rows:, :] = sums.astype(bf16)
    x = tokens_ref[...].astype(f32)
    factor = lax.rsqrt(jnp.mean(x * x, axis=1, keepdims=True) + eps)
    unit = x * factor
    scaled = total * gain_ref[...]
    pulled = (scaled - unit * jnp.mean(scaled * unit, axis=1, keepdims=True)) * factor
    grad_ref[...] = (resid_grad_ref[...] + pulled).astype(bf16)


def by_core(own_ref, other_ref, rows, columns, value):
    core = lax.axis_index("ctx") % 2
    split = value.reshape(value.shape[0] // LANES, 2, LANES // 2, value.shape[1])
    even = split[:, 0].reshape(-1, value.shape[1])
    odd = split[:, 1].reshape(-1, value.shape[1])
    own_ref[rows, columns] = jnp.where(core == 0, even, odd).astype(bf16)
    other_ref[rows, columns] = jnp.where(core == 0, odd, even).astype(bf16)


def weights_kernel(normed_ref, pair_ref, dy_ref, hidden_ref, feed_ref):
    step = 512
    wide = pair_ref.shape[1]
    for start in range(0, normed_ref.shape[1], step):
        columns = slice(start, start + step)
        feed_ref[columns, :wide] = t_dot(normed_ref[:, columns], pair_ref[...]).astype(bf16)
        feed_ref[columns, wide:] = t_dot(dy_ref[:, columns], hidden_ref[...]).astype(bf16)


def grads_kernel(normed_ref, pre_grad_ref, own_ref, other_ref):
    rows = slice(0, own_ref.shape[0])
    wide = pre_grad_ref.shape[1]
    by_core(own_ref, other_ref, rows, slice(0, wide), t_dot(normed_ref[...], pre_grad_ref[...]))


def merge_kernel(own_ref, moved_ref, last_ref, last_moved_ref, sent_ref):
    peers = sent_ref.shape[0]
    rows = own_ref.shape[0]
    part = rows // peers

    def both(first, second):
        return (first.astype(f32) + second.astype(f32)).astype(bf16)

    grads = both(own_ref[...], moved_ref[...])
    sent_ref[:, :part, : 2 * LANES] = grads.reshape(peers, part, 2 * LANES)
    last = both(last_ref[:rows, :LANES], last_moved_ref[:rows, :LANES])
    sent_ref[:, :part, 2 * LANES :] = last.reshape(peers, part, LANES)
    sums = both(last_ref[rows:, :], last_moved_ref[rows:, :])
    for peer in range(peers):
        sent_ref[peer, part:, :] = sums


def total_kernel(recv_ref, query_ref, key_ref, value_ref, out_ref, first_ref, second_ref, heads_ref):
    part = query_ref.shape[0]
    total = recv_ref[0].astype(f32)
    for peer in range(1, recv_ref.shape[0]):
        total = total + recv_ref[peer].astype(f32)
    query_ref[...] = total[:part, :LANES]
    key_ref[...] = total[:part, LANES : LANES + HEAD]
    value_ref[...] = total[:part, LANES + HEAD : 2 * LANES]
    out_ref[...] = total[:part, 2 * LANES :]
    first_ref[...] = total[part : part + 8, :LANES]
    second_ref[...] = total[part : part + 8, LANES : 2 * LANES]
    heads_ref[...] = total[part : part + 8, 2 * LANES :]


def parts_kernel(feed_ref, gate_ref, up_ref, down_ref):
    wide = gate_ref.shape[1]
    gate_ref[...] = feed_ref[:, :wide].astype(f32)
    up_ref[...] = feed_ref[:, wide : 2 * wide].astype(f32)
    down_ref[...] = feed_ref[:, 2 * wide :].astype(f32)


def feed_kernel(
    x_ref, attended_ref, w_own_ref, w_other_ref, gain_ref, w_pair_ref, hidden_grad_ref,
    resid_ref, normed_ref, hidden_ref, pair_grad_ref, part_ref, mixed_ref, sums_ref,
    w_ref, flat_ref, all_ref,
):
    core = lax.axis_index("ctx") % 2
    mine = lax.axis_index("tp")
    width = x_ref.shape[1]
    half = width // 2
    peers, local, heads = attended_ref.shape
    w_ref[core] = w_own_ref[...]
    w_ref[1 - core] = w_other_ref[...]
    rows = 256
    wide = hidden_ref.shape[1]
    gain = gain_ref[...]
    total = jnp.zeros((1, width), f32)
    for start in range(0, local, rows):
        here = pl.ds(start, rows)
        for peer in range(peers):
            flat_ref[:, peer * heads : (peer + 1) * heads] = attended_ref[peer, here, :]
        flat = flat_ref[...]
        for side in range(2):
            columns = pl.ds(side * half, half)
            all_ref[here, columns] = x_ref[here, columns].astype(f32) + dot(flat, w_ref[side])
        resid = all_ref[here, :]
        factor = lax.rsqrt(jnp.mean(resid * resid, axis=1, keepdims=True) + eps)
        normed = (resid * factor * gain).astype(bf16)
        normed_ref[here, :] = normed
        pair = dot(normed, w_pair_ref[...])
        gate, up = pair[:, :wide], pair[:, wide:]
        hidden_grad = hidden_grad_ref[here, :]
        sigma = 1.0 / (1.0 + jnp.exp(-gate))
        swish = gate * sigma
        hidden_ref[here, :] = (swish * up).astype(bf16)
        gate_grad = (hidden_grad * up * sigma * (1.0 + gate * (1.0 - sigma))).astype(bf16)
        pair_grad_ref[here, :wide] = gate_grad
        pair_grad_ref[here, wide:] = (hidden_grad * swish).astype(bf16)
        pulled = dot_t(pair_grad_ref[here, :], w_pair_ref[...])
        unit = all_ref[here, :] * factor
        total = total + jnp.sum(pulled * unit, axis=0, keepdims=True)
        scaled = pulled * gain
        part = (scaled - unit * jnp.mean(scaled * unit, axis=1, keepdims=True)) * factor
        part = part.astype(bf16)
        part_ref[here, :] = part
        mixed = dot_t(part[:, :half], w_ref[0]) + dot_t(part[:, half:], w_ref[1])
        mixed = mixed.astype(bf16)
        for peer in range(peers):
            mixed_ref[peer, here, :] = mixed[:, peer * heads : (peer + 1) * heads]
    sums_ref[...] = total
    resid_ref[...] = all_ref[block_rows(mine, local // peers), :]


def turning(positions, span_order, me, span):
    table = positions.reshape(-1, span)
    own = [lax.dynamic_index_in_dim(table, span_order[me * 2 + k], 0, False) for k in range(2)]
    places = jnp.concatenate(own).astype(f32)
    freqs = theta ** (-(jnp.arange(HEAD // 2, dtype=f32) * 2.0 / HEAD))
    turned = places[:, None] * freqs[None, :]
    cosine, sine = jnp.cos(turned), jnp.sin(turned)
    return (
        jnp.concatenate([cosine] * 4, axis=1),
        jnp.concatenate([-sine, sine, -sine, sine], axis=1),
    )


def per_device(
    tokens, cotangent, positions, span_order, first_gain, w_query, w_key, w_value,
    query_gain, key_gain, w_out, second_gain, w_gate, w_up, w_down,
):
    ctx_count = lax.axis_size("ctx")
    tp_count = lax.axis_size("tp")
    me = lax.axis_index("ctx")
    mine = lax.axis_index("tp")
    part, width = tokens.shape
    local = part * tp_count
    span = local // 2
    half = ctx_count // 2
    heads = w_out.shape[0]
    hidden_width = w_gate.shape[1]
    same_core = [[2 * k + core for k in range(half)] for core in range(2)]
    other_core = [(k, k ^ 1) for k in range(ctx_count)]
    shape = jax.ShapeDtypeStruct
    slots = pltpu.SMEM((ctx_count + 1,), jnp.int32)

    x_all = spread(tokens, "tp", tp_count).reshape(local, width)
    w_half = lax.dynamic_slice_in_dim(w_out, (me % 2) * (width // 2), width // 2, 1)
    w_half = jnp.broadcast_to(w_half[None], (tp_count, heads, width // 2))
    w_qkv = jnp.concatenate([w_query, w_key, w_value], axis=1)
    cosine, sine = turning(positions, span_order, me, span)
    head_gain = jnp.stack(
        [jnp.concatenate([query_gain, query_gain]), jnp.concatenate([key_gain, jnp.ones_like(key_gain)])]
    )

    x_all, cotangent, w_qkv, cosine, sine, head_gain = lax.optimization_barrier(
        (x_all, cotangent, w_qkv, cosine, sine, head_gain)
    )
    dy_all = lax.all_gather(cotangent, "tp", axis=0, tiled=True)

    by_span = lambda rows, cols: pl.BlockSpec((rows, cols), lambda k: (k, 0))
    whole = lambda a: pl.BlockSpec(a.shape, lambda k: (0, 0))
    gain_row = first_gain.reshape(1, width)
    normed, pre, query, kv = call(
        project_kernel,
        (
            shape((local, width), bf16),
            shape((local, 2 * LANES), f32),
            shape((local, LANES), bf16),
            shape((half, local, LANES), bf16),
        ),
        grid=(2,),
        in_specs=[
            by_span(span, width), whole(gain_row), whole(w_qkv), whole(head_gain),
            by_span(span, LANES), by_span(span, LANES),
        ],
        out_specs=(
            by_span(span, width), by_span(span, 2 * LANES), by_span(span, LANES),
            pl.BlockSpec((half, span, LANES), lambda k: (0, k, 0)),
        ),
        name="project",
    )(x_all, gain_row, w_qkv, head_gain, cosine, sine)

    query_other = lax.ppermute(query, "ctx", other_core)
    kv_all = exchange(kv, "ctx", same_core).reshape(half * local, LANES)
    w_pair = jnp.concatenate([w_gate, w_up], axis=1)
    kv_all, w_pair, w_half = lax.optimization_barrier((kv_all, w_pair, w_half))
    w_out_own = exchange(w_half, "tp").reshape(width, width // 2)
    acc, sent = call(
        attend_kernel,
        (shape((2 * local, LANES), f32), shape((2 * local, LANES), bf16)),
        in_specs=[in_smem, *in_vmem(3)],
        out_specs=tuple(in_vmem(2)),
        scratch_shapes=[
            slots, pltpu.VMEM((2 * span, LANES), bf16), pltpu.VMEM((2 * local, LANES), f32)
        ],
        cost_estimate=pl.CostEstimate(flops=8 * 10**9, bytes_accessed=2**21, transcendentals=2**23),
        name="attend",
    )(span_order, query, query_other, kv_all)
    out, attended_wide, qb = call(
        finish_kernel,
        (
            shape((2 * local, LANES), f32),
            shape((tp_count, local, LANES), bf16),
            shape((2 * local, LANES), bf16),
        ),
        in_specs=in_vmem(3),
        out_specs=tuple(in_vmem(3)),
        name="finish",
    )(acc, lax.ppermute(sent, "ctx", other_core), query)
    qb_other = lax.ppermute(qb, "ctx", other_core)
    attended_wide, w_out_own = lax.optimization_barrier((attended_wide, w_out_own))
    w_out_other = lax.ppermute(w_out_own, "ctx", other_core)

    attended_all = exchange(attended_wide, "tp")
    hidden_grad = dot_t(dy_all, w_down)
    mixed_base = dot_t(dy_all, w_out)
    resid, normed_two, hidden, pair_grad, resid_part, mixed_part, second_sum = call(
        feed_kernel,
        (
            shape((part, width), f32),
            shape((local, width), bf16),
            shape((local, hidden_width), bf16),
            shape((local, 2 * hidden_width), bf16),
            shape((local, width), bf16),
            shape((tp_count, local, heads), bf16),
            shape((1, width), f32),
        ),
        in_specs=in_vmem(7),
        out_specs=tuple(in_vmem(7)),
        scratch_shapes=[
            pltpu.VMEM((2, tp_count * heads, width // 2), bf16),
            pltpu.VMEM((256, tp_count * heads), bf16),
            pltpu.VMEM((local, width), f32),
        ],
        cost_estimate=pl.CostEstimate(flops=5 * 10**9, bytes_accessed=2**23, transcendentals=2**18),
        name="feed",
    )(
        x_all, attended_all, w_out_own, w_out_other, second_gain.reshape(1, width), w_pair,
        hidden_grad,
    )
    mixed_recv = exchange(mixed_part, "tp")

    feed = call(
        weights_kernel,
        shape((width, 3 * hidden_width), bf16),
        in_specs=in_vmem(4),
        out_specs=pl.BlockSpec(memory_space=pltpu.VMEM),
        name="weights",
    )(normed_two, pair_grad, dy_all, hidden)
    feed = lax.psum_scatter(feed, "ctx", scatter_dimension=0, tiled=True)
    down = dot(hidden, w_down).astype(bf16)
    rows_sent = jnp.concatenate([resid_part, down], axis=1).reshape(tp_count, part, 2 * width)
    rows_recv = exchange(rows_sent, "tp")

    dx = call(
        prepare_kernel,
        shape((2 * local, LANES), bf16),
        in_specs=in_vmem(3),
        out_specs=pl.BlockSpec(memory_space=pltpu.VMEM),
        name="prepare",
    )(mixed_base, mixed_recv, out)
    dx_other = lax.ppermute(dx, "ctx", other_core)
    keys_shape = (half * local, LANES)
    halves = [pltpu.VMEM((2 * span, LANES), bf16)] * 2
    pull_cost = pl.CostEstimate(flops=20 * 10**9, bytes_accessed=2**22, transcendentals=2**22)
    dkv_start, dq = call(
        partial(pull_kernel, False),
        (shape(keys_shape, f32), shape((local, LANES), f32)),
        in_specs=[in_smem, *in_vmem(3)],
        out_specs=tuple(in_vmem(2)),
        scratch_shapes=[slots, *halves, pltpu.VMEM((2 * span, LANES), f32)],
        cost_estimate=pull_cost,
        name="pull_own",
    )(span_order, kv_all, qb, dx)
    dkv, dq_other = call(
        partial(pull_kernel, True),
        (shape(keys_shape, bf16), shape((local, LANES), bf16)),
        in_specs=[in_smem, *in_vmem(4)],
        out_specs=tuple(in_vmem(2)),
        scratch_shapes=[
            slots, *halves, pltpu.VMEM(keys_shape, f32), pltpu.VMEM((2 * span, LANES), f32)
        ],
        cost_estimate=pull_cost,
        name="pull_other",
    )(span_order, kv_all, qb_other, dx_other, dkv_start)
    dkv, rows_recv = lax.optimization_barrier((dkv, rows_recv))
    resid_grad, block_out = call(
        rows_kernel,
        (shape((part, width), f32), shape((part, width), bf16)),
        in_specs=in_vmem(3),
        out_specs=tuple(in_vmem(2)),
        name="rows",
    )(rows_recv, cotangent, resid)
    dq_recv = lax.ppermute(dq_other, "ctx", other_core)
    dkv_recv = exchange(dkv.reshape(half, local, LANES), "ctx", same_core)

    pre_grad, sent = call(
        back_kernel,
        (shape((local, 2 * LANES), bf16), shape((tp_count, 2 * part + 16, width), bf16)),
        in_specs=in_vmem(12),
        out_specs=tuple(in_vmem(2)),
        name="back",
    )(dq, dq_recv, dkv_recv, pre, head_gain, cosine, sine, w_qkv, normed, gain_row, second_sum, resid_grad)
    recv = exchange(sent, "tp")
    grads_shape = shape((width // 2, 2 * LANES), bf16)
    grads, grads_sent = call(
        grads_kernel,
        (grads_shape, grads_shape),
        in_specs=in_vmem(2),
        out_specs=tuple(in_vmem(2)),
        name="grads",
    )(normed, pre_grad)
    grads_moved = lax.ppermute(grads_sent, "ctx", other_core)
    attended = attended_wide[0]
    recv, grads, grads_moved, attended = lax.optimization_barrier(
        (recv, grads, grads_moved, attended)
    )
    last_shape = shape((width // 2 + 16, 3 * LANES), bf16)
    grad_tokens, last, last_sent = call(
        tokens_kernel,
        (shape((part, width), bf16), last_shape, last_shape),
        in_specs=in_vmem(5),
        out_specs=tuple(in_vmem(3)),
        scratch_shapes=[pltpu.VMEM((local, width), bf16)],
        name="tokens",
    )(recv, tokens, gain_row, resid_grad, attended)
    sent = call(
        merge_kernel,
        shape((half, width // ctx_count + 16, 3 * LANES), bf16),
        in_specs=in_vmem(4),
        out_specs=pl.BlockSpec(memory_space=pltpu.VMEM),
        name="merge",
    )(grads, grads_moved, last, lax.ppermute(last_sent, "ctx", other_core))
    own_rows = width // ctx_count
    grad_query, grad_key, grad_value, grad_out, first_sum, second_sum, head_sums = call(
        total_kernel,
        (
            shape((own_rows, LANES), f32),
            shape((own_rows, HEAD), f32),
            shape((own_rows, HEAD), f32),
            shape((own_rows, LANES), f32),
            shape((8, LANES), f32),
            shape((8, LANES), f32),
            shape((8, LANES), f32),
        ),
        in_specs=in_vmem(1),
        out_specs=tuple(in_vmem(7)),
        name="total",
    )(exchange(sent, "ctx", same_core))
    own_shape = shape((own_rows, hidden_width), f32)
    grad_gate, grad_up, grad_down = call(
        parts_kernel,
        (own_shape, own_shape, own_shape),
        in_specs=in_vmem(1),
        out_specs=tuple(in_vmem(3)),
        name="parts",
    )(feed)
    return (
        block_out,
        grad_tokens,
        first_sum.reshape(width),
        grad_query,
        grad_key,
        grad_value,
        head_sums[0, :HEAD],
        head_sums[0, HEAD:],
        grad_out.T,
        second_sum.reshape(width),
        grad_gate,
        grad_up,
        grad_down.T,
    )


def solution(mesh):
    return jax.shard_map(
        per_device,
        mesh=mesh,
        in_specs=(
            P(("ctx", "tp"), None),
            P(("ctx", "tp"), None),
            P(),
            P(),
            P(),
            P(None, "tp"),
            P(None, "tp"),
            P(None, "tp"),
            P(),
            P(),
            P("tp", None),
            P(),
            P(None, "tp"),
            P(None, "tp"),
            P("tp", None),
        ),
        out_specs=(
            P(("ctx", "tp"), None),
            P(("ctx", "tp"), None),
            P(),
            P("ctx", "tp"),
            P("ctx", "tp"),
            P("ctx", "tp"),
            P(),
            P(),
            P("tp", "ctx"),
            P(),
            P("ctx", "tp"),
            P("ctx", "tp"),
            P("tp", "ctx"),
        ),
        check_vma=False,
    )
```

```python
from functools import partial
import math

import jax
import jax.numpy as jnp
from jax import lax
from jax.experimental import pallas as pl
from jax.experimental.pallas import tpu as pltpu
from jax.sharding import PartitionSpec as P

eps = 1e-05
theta = 1000000.0
bf16 = jnp.bfloat16
f32 = jnp.float32
large = 56 * 1024 * 1024
small = 24 * 1024 * 1024
log2e = math.log2(math.e)
HEAD = 64
LANES = 128


def dot(a, b):
    return jnp.dot(a, b, preferred_element_type=f32)


def dot_t(a, b):
    return lax.dot_general(a, b, (((1,), (1,)), ((), ())), preferred_element_type=f32)


def t_dot(a, b):
    return lax.dot_general(a, b, (((0,), (0,)), ((), ())), preferred_element_type=f32)


def call(kernel, out_shape, vmem_bytes=small, **more):
    return pl.pallas_call(
        kernel,
        out_shape=out_shape,
        compiler_params=pltpu.CompilerParams(vmem_limit_bytes=vmem_bytes),
        **more,
    )


def in_vmem(count):
    return [pl.BlockSpec(memory_space=pltpu.VMEM)] * count


in_smem = pl.BlockSpec(memory_space=pltpu.SMEM)


def exchange(x, axis, groups=None):
    return lax.all_to_all(x, axis, 0, 0, axis_index_groups=groups, tiled=True)


def spread(x, axis, count, groups=None):
    return exchange(jnp.broadcast_to(x[None], (count, *x.shape)), axis, groups)


def left_half(shape):
    return lax.broadcasted_iota(jnp.int32, shape, 1) < HEAD


def swap_quarters(v):
    lane = lax.broadcasted_iota(jnp.int32, v.shape, 1)
    return jnp.where(lane % HEAD < HEAD // 2, pltpu.roll(v, LANES - 32, 1), pltpu.roll(v, 32, 1))


def head_mean(v, left):
    first = jnp.sum(jnp.where(left, v, 0.0), axis=1, keepdims=True)
    second = jnp.sum(jnp.where(left, 0.0, v), axis=1, keepdims=True)
    return jnp.where(left, first, second) * (1.0 / HEAD)


def project_kernel(
    x_ref, gain_ref, w_ref, head_gain_ref, cos_ref, sin_ref, normed_ref, pre_ref, query_ref, kv_ref
):
    x = x_ref[...].astype(f32)
    scaled = x * lax.rsqrt(jnp.mean(x * x, axis=1, keepdims=True) + eps)
    normed = (scaled * gain_ref[...]).astype(bf16)
    normed_ref[...] = normed
    pre = dot(normed, w_ref[...])
    pre_ref[...] = pre
    cosine, sine = cos_ref[...], sin_ref[...]
    left = left_half((x.shape[0], LANES))

    def prepared(v, gain):
        v = v * lax.rsqrt(head_mean(v * v, left) + eps) * gain
        return v * cosine + swap_quarters(v) * sine

    query = prepared(pre[:, :LANES], head_gain_ref[0:1, :])
    query_ref[...] = (query * (log2e / math.sqrt(HEAD))).astype(bf16)
    pair = pre[:, LANES:]
    key = prepared(pair, head_gain_ref[1:2, :])
    both = jnp.where(left, key, pair).astype(bf16)
    for peer in range(kv_ref.shape[0]):
        kv_ref[peer] = both


def earlier_spans(order_ref, list_ref, rank, core, blocks):
    count = jnp.int32(0)
    for block in range(blocks):
        list_ref[count] = jnp.int32(block)
        slot = ((block // 2) * 2 + core) * 2 + block % 2
        count = count + (order_ref[slot] < rank).astype(jnp.int32)
    return count


def block_rows(index, span):
    return pl.ds(pl.multiple_of(index * span, span), span)


def in_groups(count, size, body):
    whole = count // size

    def some(step, carry):
        body([step * size + k for k in range(size)])
        return carry

    lax.fori_loop(0, whole, some, 0)

    def one(step, carry):
        body([step])
        return carry

    lax.fori_loop(whole * size, count, one, 0)


def pieces(v, count):
    parts = []
    for _ in range(count):
        part = v.astype(bf16).astype(f32)
        parts.append(part)
        v = v - part
    return parts


def attend_kernel(order_ref, own_ref, other_ref, kv_ref, acc_ref, sent_ref, list_ref, qx_ref, sum_ref):
    me = lax.axis_index("ctx")
    core = me % 2
    span = own_ref.shape[0] // 2
    blocks = kv_ref.shape[0] // span
    left = left_half((span, LANES))
    lane = lax.broadcasted_iota(jnp.int32, (span, LANES), 1)
    for source in range(2):
        for slot in range(2):
            query = (own_ref, other_ref)[source][pl.ds(slot * span, span), :].astype(f32)
            for head in range(2):
                own = query if head == 0 else pltpu.roll(query, HEAD, 1)
                qx_ref[pl.ds(head * span, span), :] = jnp.where(left, own, 0.0).astype(bf16)
            rank = order_ref[(me + source * (1 - 2 * core)) * 2 + slot]
            count = earlier_spans(order_ref, list_ref, rank, core, blocks)

            def product(indices, mask=None):
                pair = jnp.concatenate([kv_ref[block_rows(k, span), :] for k in indices], axis=0)
                weights = jnp.exp2(dot_t(pair, qx_ref[...]))
                if mask is not None:
                    weights = jnp.where(mask, weights, 0.0)
                values = jnp.where(left_half(pair.shape), jnp.ones_like(pair), pair)
                return t_dot(values, weights.astype(bf16))

            if source == 0:
                row = lax.broadcasted_iota(jnp.int32, (span, 2 * span), 0)
                col = lax.broadcasted_iota(jnp.int32, (span, 2 * span), 1) % span
                sum_ref[...] = product([(me // 2) * 2 + slot], col >= row)
            else:
                sum_ref[...] = jnp.zeros_like(sum_ref)

            def add(steps):
                sum_ref[...] += product([list_ref[step] for step in steps])

            in_groups(count, 4, add)
            for head in range(2):
                part = pl.ds((slot * 2 + head) * span, span)
                acc = sum_ref[:, head * span : (head + 1) * span].T
                if source == 0:
                    acc_ref[part, :] = acc
                else:
                    high, middle, low = pieces(acc, 3)
                    packed = jnp.where(lane == 0, high, jnp.where(lane == 1, middle, low))
                    packed = jnp.where(lane < 3, packed, jnp.where(left, 0.0, acc))
                    sent_ref[part, :] = packed.astype(bf16)


def finish_kernel(acc_ref, recv_ref, query_ref, out_ref, attended_ref, qb_ref):
    span = query_ref.shape[0] // 2
    left = left_half((span, LANES))
    lane = lax.broadcasted_iota(jnp.int32, (span, LANES), 1)
    for slot in range(2):
        rows = pl.ds(slot * span, span)
        query = query_ref[rows, :].astype(f32)
        outs = []
        for head in range(2):
            part = pl.ds((slot * 2 + head) * span, span)
            recv = recv_ref[part, :].astype(f32)
            acc = acc_ref[part, :]
            total = jnp.sum(jnp.where(left, recv, 0.0), axis=1, keepdims=True)
            total = total + jnp.where(left, acc, pltpu.roll(acc, HEAD, 1))
            logs = jnp.log2(total)
            out = jnp.where(left, logs, (acc + recv) / total)
            out_ref[part, :] = out
            outs.append(out)
            high, middle, low = pieces(logs, 3)
            own = jnp.where(left, query if head == 0 else pltpu.roll(query, HEAD, 1), 0.0)
            own = jnp.where(lane == HEAD, -high, own)
            own = jnp.where(lane == HEAD + 1, -middle, own)
            own = jnp.where(lane == HEAD + 2, -low, own)
            qb_ref[part, :] = own.astype(bf16)
        both = jnp.where(left, pltpu.roll(outs[0], HEAD, 1), outs[1]).astype(bf16)
        for peer in range(attended_ref.shape[0]):
            attended_ref[peer, rows, :] = both


def prepare_kernel(base_ref, recv_ref, out_ref, dx_ref):
    span = base_ref.shape[0] // 2
    left = left_half((span, LANES))
    lane = lax.broadcasted_iota(jnp.int32, (span, LANES), 1)
    for slot in range(2):
        rows = pl.ds(slot * span, span)
        mixed = base_ref[rows, :]
        for peer in range(recv_ref.shape[0]):
            mixed = mixed + recv_ref[peer, rows, :].astype(f32)
        mixed = mixed.astype(bf16).astype(f32)
        for head in range(2):
            part = pl.ds((slot * 2 + head) * span, span)
            own = jnp.where(left, 0.0, pltpu.roll(mixed, HEAD, 1) if head == 0 else mixed)
            delta = jnp.sum(own * out_ref[part, :], axis=1, keepdims=True)
            high, low = pieces(delta, 2)
            own = jnp.where(lane == 0, -high, jnp.where(lane == 1, -low, own))
            dx_ref[part, :] = own.astype(bf16)


def pull_kernel(last, order_ref, kv_ref, qb_ref, dx_ref, *refs):
    if last:
        start_ref, out_ref, dq_out_ref, list_ref, qz_ref, dz_ref, dkv_ref, dq_ref = refs
        dkv_ref[...] = start_ref[...]
    else:
        dkv_ref, dq_out_ref, list_ref, qz_ref, dz_ref, dq_ref = refs
        dkv_ref[...] = jnp.zeros_like(dkv_ref)
    me = lax.axis_index("ctx")
    core = me % 2
    whose = me + 1 - 2 * core if last else me
    span = qb_ref.shape[0] // 4
    blocks = kv_ref.shape[0] // span
    left = left_half((span, LANES))
    one = jnp.ones((span, LANES), bf16)
    zero = jnp.zeros((2 * span, LANES), bf16)
    wide_left = left_half((2 * span, LANES))
    for slot in range(2):
        rows = pl.ds(slot * 2 * span, 2 * span)
        qz_ref[...] = jnp.where(wide_left, qb_ref[rows, :], zero)
        dz_ref[...] = jnp.where(wide_left, zero, dx_ref[rows, :])
        count = earlier_spans(order_ref, list_ref, order_ref[whose * 2 + slot], core, blocks)

        def product(index, mask=None):
            part = block_rows(index, span)
            pair = kv_ref[part, :]
            weights = jnp.exp2(dot_t(jnp.where(left, pair, one), qb_ref[rows, :]))
            if mask is not None:
                weights = jnp.where(mask, weights, 0.0)
            pulled = dot_t(jnp.where(left, one, pair), dx_ref[rows, :])
            score = (weights * pulled).astype(bf16)
            dkv_ref[part, :] += dot(score, qz_ref[...]) + dot(weights.astype(bf16), dz_ref[...])
            return t_dot(pair, score)

        if last:
            dq_ref[...] = jnp.zeros_like(dq_ref)
        else:
            row = lax.broadcasted_iota(jnp.int32, (span, 2 * span), 0)
            col = lax.broadcasted_iota(jnp.int32, (span, 2 * span), 1) % span
            dq_ref[...] = product((me // 2) * 2 + slot, col >= row)

        def add(steps):
            dq_ref[...] += sum(product(list_ref[step]) for step in steps)

        in_groups(count, 4, add)
        first, second = dq_ref[:, :span].T, dq_ref[:, span:].T
        both = jnp.where(left, first, pltpu.roll(second, HEAD, 1))
        dq_out_ref[pl.ds(slot * span, span), :] = both.astype(dq_out_ref.dtype)
    if last:
        factor = jnp.where(left_half((1, LANES)), 1.0 / log2e, 1.0)
        out_ref[...] = (dkv_ref[...] * factor).astype(bf16)


def rows_kernel(recv_ref, cotangent_ref, resid_ref, grad_ref, block_ref):
    width = resid_ref.shape[1]
    total = recv_ref[0].astype(f32)
    for peer in range(1, recv_ref.shape[0]):
        total = total + recv_ref[peer].astype(f32)
    grad_ref[...] = cotangent_ref[...].astype(f32) + total[:, :width]
    block_ref[...] = (resid_ref[...] + total[:, width:]).astype(bf16)


def as_rows(v):
    return jnp.concatenate([v[:, k : k + LANES] for k in range(0, v.shape[1], LANES)], axis=0)


def back_kernel(
    dq_ref, dq_recv_ref, recv_ref, pre_ref, head_gain_ref, cos_ref, sin_ref, w_ref, normed_ref,
    gain_ref, second_ref, grad_ref, pre_grad_ref, sent_ref,
):
    span = cos_ref.shape[0] // 2
    peers, _, width = sent_ref.shape
    part = 2 * span // peers
    left = left_half((span, LANES))

    def pulled(grad, pre, gain, cosine, sine):
        turned = grad * cosine - swap_quarters(grad) * sine
        factor = lax.rsqrt(head_mean(pre * pre, left) + eps)
        unit = pre * factor
        sums = jnp.sum(turned * unit, axis=0, keepdims=True)
        scaled = turned * gain
        return (scaled - unit * head_mean(scaled * unit, left)) * factor, sums

    totals = [0.0, 0.0, 0.0]
    for slot in range(2):
        rows = pl.ds(slot * span, span)
        cosine, sine = cos_ref[rows, :], sin_ref[rows, :]
        grad = (dq_ref[rows, :] + dq_recv_ref[rows, :].astype(f32)) * (1.0 / math.sqrt(HEAD))
        pair = recv_ref[0, rows, :].astype(f32)
        for peer in range(1, recv_ref.shape[0]):
            pair = pair + recv_ref[peer, rows, :].astype(f32)
        query, sums = pulled(grad, pre_ref[rows, :LANES], head_gain_ref[0:1, :], cosine, sine)
        totals[0] = totals[0] + sums
        key, sums = pulled(
            jnp.where(left, pair, 0.0), pre_ref[rows, LANES:], head_gain_ref[1:2, :], cosine, sine
        )
        totals[1] = totals[1] + sums
        pre_grad_ref[rows, :LANES] = query.astype(bf16)
        pre_grad_ref[rows, LANES:] = jnp.where(left, key, pair).astype(bf16)
        normed_part = dot_t(pre_grad_ref[rows, :], w_ref[...])
        totals[2] = totals[2] + jnp.sum(
            normed_part * normed_ref[rows, :].astype(f32), axis=0, keepdims=True
        )
        sent = normed_part.astype(bf16).reshape(peers // 2, part, width)
        sent_ref[slot * (peers // 2) : (slot + 1) * (peers // 2), :part, :] = sent
    folded = totals[0] + pltpu.roll(totals[0], HEAD, 1)
    heads = jnp.where(left_half((1, LANES)), folded, pltpu.roll(totals[1], HEAD, 1))
    sums = jnp.concatenate(
        [as_rows(totals[2] / gain_ref[...]), as_rows(second_ref[...]), jnp.broadcast_to(heads, (8, LANES))],
        axis=1,
    )
    sums = jnp.concatenate([sums, jnp.zeros_like(sums)], axis=0).astype(bf16)
    for peer in range(peers):
        sent_ref[peer, part : 2 * part, :] = grad_ref[...].astype(bf16)
        sent_ref[peer, 2 * part :, : 3 * LANES] = sums
        sent_ref[peer, 2 * part :, 3 * LANES :] = jnp.zeros((16, width - 3 * LANES), bf16)


def tokens_kernel(
    recv_ref, tokens_ref, gain_ref, resid_grad_ref, attended_ref, grad_ref, own_ref, other_ref,
    flat_ref,
):
    part = tokens_ref.shape[0]
    rows = own_ref.shape[0] - 16
    total = recv_ref[0, :part].astype(f32)
    sums = recv_ref[0, 2 * part :, : 3 * LANES].astype(f32)
    for peer in range(1, recv_ref.shape[0]):
        total = total + recv_ref[peer, :part].astype(f32)
        sums = sums + recv_ref[peer, 2 * part :, : 3 * LANES].astype(f32)
    for peer in range(recv_ref.shape[0]):
        flat_ref[peer * part : (peer + 1) * part, :] = recv_ref[peer, part : 2 * part]
    by_core(
        own_ref, other_ref, slice(0, rows), slice(0, LANES), t_dot(flat_ref[...], attended_ref[...])
    )
    for target in (own_ref, other_ref):
        target[:rows, LANES:] = jnp.zeros((rows, 2 * LANES), bf16)
        target[rows:, :] = sums.astype(bf16)
    x = tokens_ref[...].astype(f32)
    factor = lax.rsqrt(jnp.mean(x * x, axis=1, keepdims=True) + eps)
    unit = x * factor
    scaled = total * gain_ref[...]
    pulled = (scaled - unit * jnp.mean(scaled * unit, axis=1, keepdims=True)) * factor
    grad_ref[...] = (resid_grad_ref[...] + pulled).astype(bf16)


def by_core(own_ref, other_ref, rows, columns, value):
    core = lax.axis_index("ctx") % 2
    split = value.reshape(value.shape[0] // LANES, 2, LANES // 2, value.shape[1])
    even = split[:, 0].reshape(-1, value.shape[1])
    odd = split[:, 1].reshape(-1, value.shape[1])
    own_ref[rows, columns] = jnp.where(core == 0, even, odd).astype(bf16)
    other_ref[rows, columns] = jnp.where(core == 0, odd, even).astype(bf16)


def weights_kernel(normed_ref, pair_ref, dy_ref, hidden_ref, feed_ref):
    step = 512
    wide = pair_ref.shape[1]
    for start in range(0, normed_ref.shape[1], step):
        columns = slice(start, start + step)
        feed_ref[columns, :wide] = t_dot(normed_ref[:, columns], pair_ref[...]).astype(bf16)
        feed_ref[columns, wide:] = t_dot(dy_ref[:, columns], hidden_ref[...]).astype(bf16)


def grads_kernel(normed_ref, pre_grad_ref, own_ref, other_ref):
    rows = slice(0, own_ref.shape[0])
    wide = pre_grad_ref.shape[1]
    by_core(own_ref, other_ref, rows, slice(0, wide), t_dot(normed_ref[...], pre_grad_ref[...]))


def merge_kernel(own_ref, moved_ref, last_ref, last_moved_ref, sent_ref):
    peers = sent_ref.shape[0]
    rows = own_ref.shape[0]
    part = rows // peers

    def both(first, second):
        return (first.astype(f32) + second.astype(f32)).astype(bf16)

    grads = both(own_ref[...], moved_ref[...])
    sent_ref[:, :part, : 2 * LANES] = grads.reshape(peers, part, 2 * LANES)
    last = both(last_ref[:rows, :LANES], last_moved_ref[:rows, :LANES])
    sent_ref[:, :part, 2 * LANES :] = last.reshape(peers, part, LANES)
    sums = both(last_ref[rows:, :], last_moved_ref[rows:, :])
    for peer in range(peers):
        sent_ref[peer, part:, :] = sums


def total_kernel(recv_ref, query_ref, key_ref, value_ref, out_ref, first_ref, second_ref, heads_ref):
    part = query_ref.shape[0]
    total = recv_ref[0].astype(f32)
    for peer in range(1, recv_ref.shape[0]):
        total = total + recv_ref[peer].astype(f32)
    query_ref[...] = total[:part, :LANES]
    key_ref[...] = total[:part, LANES : LANES + HEAD]
    value_ref[...] = total[:part, LANES + HEAD : 2 * LANES]
    out_ref[...] = total[:part, 2 * LANES :]
    first_ref[...] = total[part : part + 8, :LANES]
    second_ref[...] = total[part : part + 8, LANES : 2 * LANES]
    heads_ref[...] = total[part : part + 8, 2 * LANES :]


def parts_kernel(feed_ref, gate_ref, up_ref, down_ref):
    wide = gate_ref.shape[1]
    gate_ref[...] = feed_ref[:, :wide].astype(f32)
    up_ref[...] = feed_ref[:, wide : 2 * wide].astype(f32)
    down_ref[...] = feed_ref[:, 2 * wide :].astype(f32)


def feed_kernel(
    x_ref, attended_ref, w_own_ref, w_other_ref, gain_ref, w_pair_ref, hidden_grad_ref,
    resid_ref, normed_ref, hidden_ref, pair_grad_ref, part_ref, mixed_ref, sums_ref,
    w_ref, flat_ref, all_ref,
):
    core = lax.axis_index("ctx") % 2
    mine = lax.axis_index("tp")
    width = x_ref.shape[1]
    half = width // 2
    peers, local, heads = attended_ref.shape
    w_ref[core] = w_own_ref[...]
    w_ref[1 - core] = w_other_ref[...]
    rows = 256
    wide = hidden_ref.shape[1]
    gain = gain_ref[...]
    total = jnp.zeros((1, width), f32)
    for start in range(0, local, rows):
        here = pl.ds(start, rows)
        for peer in range(peers):
            flat_ref[:, peer * heads : (peer + 1) * heads] = attended_ref[peer, here, :]
        flat = flat_ref[...]
        for side in range(2):
            columns = pl.ds(side * half, half)
            all_ref[here, columns] = x_ref[here, columns].astype(f32) + dot(flat, w_ref[side])
        resid = all_ref[here, :]
        factor = lax.rsqrt(jnp.mean(resid * resid, axis=1, keepdims=True) + eps)
        normed = (resid * factor * gain).astype(bf16)
        normed_ref[here, :] = normed
        pair = dot(normed, w_pair_ref[...])
        gate, up = pair[:, :wide], pair[:, wide:]
        hidden_grad = hidden_grad_ref[here, :]
        sigma = 1.0 / (1.0 + jnp.exp(-gate))
        swish = gate * sigma
        hidden_ref[here, :] = (swish * up).astype(bf16)
        gate_grad = (hidden_grad * up * sigma * (1.0 + gate * (1.0 - sigma))).astype(bf16)
        pair_grad_ref[here, :wide] = gate_grad
        pair_grad_ref[here, wide:] = (hidden_grad * swish).astype(bf16)
        pulled = dot_t(pair_grad_ref[here, :], w_pair_ref[...])
        unit = all_ref[here, :] * factor
        total = total + jnp.sum(pulled * unit, axis=0, keepdims=True)
        scaled = pulled * gain
        part = (scaled - unit * jnp.mean(scaled * unit, axis=1, keepdims=True)) * factor
        part = part.astype(bf16)
        part_ref[here, :] = part
        mixed = dot_t(part[:, :half], w_ref[0]) + dot_t(part[:, half:], w_ref[1])
        mixed = mixed.astype(bf16)
        for peer in range(peers):
            mixed_ref[peer, here, :] = mixed[:, peer * heads : (peer + 1) * heads]
    sums_ref[...] = total
    resid_ref[...] = all_ref[block_rows(mine, local // peers), :]


def turning(positions, span_order, me, span):
    table = positions.reshape(-1, span)
    own = [lax.dynamic_index_in_dim(table, span_order[me * 2 + k], 0, False) for k in range(2)]
    places = jnp.concatenate(own).astype(f32)
    freqs = theta ** (-(jnp.arange(HEAD // 2, dtype=f32) * 2.0 / HEAD))
    turned = places[:, None] * freqs[None, :]
    cosine, sine = jnp.cos(turned), jnp.sin(turned)
    return (
        jnp.concatenate([cosine] * 4, axis=1),
        jnp.concatenate([-sine, sine, -sine, sine], axis=1),
    )


def per_device(
    tokens, cotangent, positions, span_order, first_gain, w_query, w_key, w_value,
    query_gain, key_gain, w_out, second_gain, w_gate, w_up, w_down,
):
    ctx_count = lax.axis_size("ctx")
    tp_count = lax.axis_size("tp")
    me = lax.axis_index("ctx")
    mine = lax.axis_index("tp")
    part, width = tokens.shape
    local = part * tp_count
    span = local // 2
    half = ctx_count // 2
    heads = w_out.shape[0]
    hidden_width = w_gate.shape[1]
    same_core = [[2 * k + core for k in range(half)] for core in range(2)]
    other_core = [(k, k ^ 1) for k in range(ctx_count)]
    shape = jax.ShapeDtypeStruct
    slots = pltpu.SMEM((ctx_count + 1,), jnp.int32)

    x_all = spread(tokens, "tp", tp_count).reshape(local, width)
    w_half = lax.dynamic_slice_in_dim(w_out, (me % 2) * (width // 2), width // 2, 1)
    w_half = jnp.broadcast_to(w_half[None], (tp_count, heads, width // 2))
    w_qkv = jnp.concatenate([w_query, w_key, w_value], axis=1)
    cosine, sine = turning(positions, span_order, me, span)
    head_gain = jnp.stack(
        [jnp.concatenate([query_gain, query_gain]), jnp.concatenate([key_gain, jnp.ones_like(key_gain)])]
    )

    x_all, w_qkv, cosine, sine, head_gain = lax.optimization_barrier(
        (x_all, w_qkv, cosine, sine, head_gain)
    )
    dy_all = lax.all_gather(cotangent, "tp", axis=0, tiled=True)

    by_span = lambda rows, cols: pl.BlockSpec((rows, cols), lambda k: (k, 0))
    whole = lambda a: pl.BlockSpec(a.shape, lambda k: (0, 0))
    gain_row = first_gain.reshape(1, width)
    normed, pre, query, kv = call(
        project_kernel,
        (
            shape((local, width), bf16),
            shape((local, 2 * LANES), f32),
            shape((local, LANES), bf16),
            shape((half, local, LANES), bf16),
        ),
        grid=(2,),
        in_specs=[
            by_span(span, width), whole(gain_row), whole(w_qkv), whole(head_gain),
            by_span(span, LANES), by_span(span, LANES),
        ],
        out_specs=(
            by_span(span, width), by_span(span, 2 * LANES), by_span(span, LANES),
            pl.BlockSpec((half, span, LANES), lambda k: (0, k, 0)),
        ),
        name="project",
    )(x_all, gain_row, w_qkv, head_gain, cosine, sine)

    query_other = lax.ppermute(query, "ctx", other_core)
    kv_all = exchange(kv, "ctx", same_core).reshape(half * local, LANES)
    w_pair = jnp.concatenate([w_gate, w_up], axis=1)
    kv_all, w_pair, w_half, dy_all = lax.optimization_barrier((kv_all, w_pair, w_half, dy_all))
    w_out_own = exchange(w_half, "tp").reshape(width, width // 2)
    acc, sent = call(
        attend_kernel,
        (shape((2 * local, LANES), f32), shape((2 * local, LANES), bf16)),
        in_specs=[in_smem, *in_vmem(3)],
        out_specs=tuple(in_vmem(2)),
        scratch_shapes=[
            slots, pltpu.VMEM((2 * span, LANES), bf16), pltpu.VMEM((LANES, 2 * span), f32)
        ],
        cost_estimate=pl.CostEstimate(flops=8 * 10**9, bytes_accessed=2**21, transcendentals=2**23),
        name="attend",
    )(span_order, query, query_other, kv_all)
    out, attended_wide, qb = call(
        finish_kernel,
        (
            shape((2 * local, LANES), f32),
            shape((tp_count, local, LANES), bf16),
            shape((2 * local, LANES), bf16),
        ),
        in_specs=in_vmem(3),
        out_specs=tuple(in_vmem(3)),
        name="finish",
    )(acc, lax.ppermute(sent, "ctx", other_core), query)
    qb_other = lax.ppermute(qb, "ctx", other_core)
    attended_wide, w_out_own = lax.optimization_barrier((attended_wide, w_out_own))
    w_out_other = lax.ppermute(w_out_own, "ctx", other_core)

    attended_all = exchange(attended_wide, "tp")
    hidden_grad = dot_t(dy_all, w_down)
    mixed_base = dot_t(dy_all, w_out)
    resid, normed_two, hidden, pair_grad, resid_part, mixed_part, second_sum = call(
        feed_kernel,
        (
            shape((part, width), f32),
            shape((local, width), bf16),
            shape((local, hidden_width), bf16),
            shape((local, 2 * hidden_width), bf16),
            shape((local, width), bf16),
            shape((tp_count, local, heads), bf16),
            shape((1, width), f32),
        ),
        in_specs=in_vmem(7),
        out_specs=tuple(in_vmem(7)),
        scratch_shapes=[
            pltpu.VMEM((2, tp_count * heads, width // 2), bf16),
            pltpu.VMEM((256, tp_count * heads), bf16),
            pltpu.VMEM((local, width), f32),
        ],
        cost_estimate=pl.CostEstimate(flops=5 * 10**9, bytes_accessed=2**23, transcendentals=2**18),
        name="feed",
        vmem_bytes=large,
    )(
        x_all, attended_all, w_out_own, w_out_other, second_gain.reshape(1, width), w_pair,
        hidden_grad,
    )
    mixed_recv = exchange(mixed_part, "tp")

    feed = call(
        weights_kernel,
        shape((width, 3 * hidden_width), bf16),
        in_specs=in_vmem(4),
        out_specs=pl.BlockSpec(memory_space=pltpu.VMEM),
        name="weights",
        vmem_bytes=large,
    )(normed_two, pair_grad, dy_all, hidden)
    feed = lax.psum_scatter(feed, "ctx", scatter_dimension=0, tiled=True)
    down = dot(hidden, w_down).astype(bf16)
    rows_sent = jnp.concatenate([resid_part, down], axis=1).reshape(tp_count, part, 2 * width)
    rows_recv = exchange(rows_sent, "tp")

    dx = call(
        prepare_kernel,
        shape((2 * local, LANES), bf16),
        in_specs=in_vmem(3),
        out_specs=pl.BlockSpec(memory_space=pltpu.VMEM),
        name="prepare",
    )(mixed_base, mixed_recv, out)
    dx_other = lax.ppermute(dx, "ctx", other_core)
    keys_shape = (half * local, LANES)
    halves = [pltpu.VMEM((2 * span, LANES), bf16)] * 2
    pull_cost = pl.CostEstimate(flops=20 * 10**9, bytes_accessed=2**22, transcendentals=2**22)
    dkv_start, dq = call(
        partial(pull_kernel, False),
        (shape(keys_shape, f32), shape((local, LANES), f32)),
        in_specs=[in_smem, *in_vmem(3)],
        out_specs=tuple(in_vmem(2)),
        scratch_shapes=[slots, *halves, pltpu.VMEM((LANES, 2 * span), f32)],
        cost_estimate=pull_cost,
        name="pull_own",
    )(span_order, kv_all, qb, dx)
    dkv, dq_other = call(
        partial(pull_kernel, True),
        (shape(keys_shape, bf16), shape((local, LANES), bf16)),
        in_specs=[in_smem, *in_vmem(4)],
        out_specs=tuple(in_vmem(2)),
        scratch_shapes=[
            slots, *halves, pltpu.VMEM(keys_shape, f32), pltpu.VMEM((LANES, 2 * span), f32)
        ],
        cost_estimate=pull_cost,
        name="pull_other",
    )(span_order, kv_all, qb_other, dx_other, dkv_start)
    dkv, rows_recv = lax.optimization_barrier((dkv, rows_recv))
    resid_grad, block_out = call(
        rows_kernel,
        (shape((part, width), f32), shape((part, width), bf16)),
        in_specs=in_vmem(3),
        out_specs=tuple(in_vmem(2)),
        name="rows",
    )(rows_recv, cotangent, resid)
    dq_recv = lax.ppermute(dq_other, "ctx", other_core)
    dkv_recv = exchange(dkv.reshape(half, local, LANES), "ctx", same_core)

    pre_grad, sent = call(
        back_kernel,
        (shape((local, 2 * LANES), bf16), shape((tp_count, 2 * part + 16, width), bf16)),
        in_specs=in_vmem(12),
        out_specs=tuple(in_vmem(2)),
        name="back",
        vmem_bytes=large,
    )(dq, dq_recv, dkv_recv, pre, head_gain, cosine, sine, w_qkv, normed, gain_row, second_sum, resid_grad)
    recv = exchange(sent, "tp")
    grads_shape = shape((width // 2, 2 * LANES), bf16)
    grads, grads_sent = call(
        grads_kernel,
        (grads_shape, grads_shape),
        in_specs=in_vmem(2),
        out_specs=tuple(in_vmem(2)),
        name="grads",
    )(normed, pre_grad)
    grads_moved = lax.ppermute(grads_sent, "ctx", other_core)
    attended = attended_wide[0]
    recv, grads, grads_moved, attended = lax.optimization_barrier(
        (recv, grads, grads_moved, attended)
    )
    last_shape = shape((width // 2 + 16, 3 * LANES), bf16)
    grad_tokens, last, last_sent = call(
        tokens_kernel,
        (shape((part, width), bf16), last_shape, last_shape),
        in_specs=in_vmem(5),
        out_specs=tuple(in_vmem(3)),
        scratch_shapes=[pltpu.VMEM((local, width), bf16)],
        name="tokens",
    )(recv, tokens, gain_row, resid_grad, attended)
    sent = call(
        merge_kernel,
        shape((half, width // ctx_count + 16, 3 * LANES), bf16),
        in_specs=in_vmem(4),
        out_specs=pl.BlockSpec(memory_space=pltpu.VMEM),
        name="merge",
    )(grads, grads_moved, last, lax.ppermute(last_sent, "ctx", other_core))
    own_rows = width // ctx_count
    grad_query, grad_key, grad_value, grad_out, first_sum, second_sum, head_sums = call(
        total_kernel,
        (
            shape((own_rows, LANES), f32),
            shape((own_rows, HEAD), f32),
            shape((own_rows, HEAD), f32),
            shape((own_rows, LANES), f32),
            shape((8, LANES), f32),
            shape((8, LANES), f32),
            shape((8, LANES), f32),
        ),
        in_specs=in_vmem(1),
        out_specs=tuple(in_vmem(7)),
        name="total",
    )(exchange(sent, "ctx", same_core))
    own_shape = shape((own_rows, hidden_width), f32)
    grad_gate, grad_up, grad_down = call(
        parts_kernel,
        (own_shape, own_shape, own_shape),
        in_specs=in_vmem(1),
        out_specs=tuple(in_vmem(3)),
        name="parts",
    )(feed)
    return (
        block_out,
        grad_tokens,
        first_sum.reshape(width),
        grad_query,
        grad_key,
        grad_value,
        head_sums[0, :HEAD],
        head_sums[0, HEAD:],
        grad_out.T,
        second_sum.reshape(width),
        grad_gate,
        grad_up,
        grad_down.T,
    )


def solution(mesh):
    return jax.shard_map(
        per_device,
        mesh=mesh,
        in_specs=(
            P(("ctx", "tp"), None),
            P(("ctx", "tp"), None),
            P(),
            P(),
            P(),
            P(None, "tp"),
            P(None, "tp"),
            P(None, "tp"),
            P(),
            P(),
            P("tp", None),
            P(),
            P(None, "tp"),
            P(None, "tp"),
            P("tp", None),
        ),
        out_specs=(
            P(("ctx", "tp"), None),
            P(("ctx", "tp"), None),
            P(),
            P("ctx", "tp"),
            P("ctx", "tp"),
            P("ctx", "tp"),
            P(),
            P(),
            P("tp", "ctx"),
            P(),
            P("ctx", "tp"),
            P("ctx", "tp"),
            P("tp", "ctx"),
        ),
        check_vma=False,
    )
```

```python
from functools import partial
import math

import jax
import jax.numpy as jnp
from jax import lax
from jax.experimental import pallas as pl
from jax.experimental.pallas import tpu as pltpu
from jax.sharding import PartitionSpec as P

eps = 1e-05
theta = 1000000.0
bf16 = jnp.bfloat16
f32 = jnp.float32
large = 56 * 1024 * 1024
small = 24 * 1024 * 1024
log2e = math.log2(math.e)
HEAD = 64
LANES = 128


def dot(a, b):
    return jnp.dot(a, b, preferred_element_type=f32)


def dot_t(a, b):
    return lax.dot_general(a, b, (((1,), (1,)), ((), ())), preferred_element_type=f32)


def t_dot(a, b):
    return lax.dot_general(a, b, (((0,), (0,)), ((), ())), preferred_element_type=f32)


def call(kernel, out_shape, vmem_bytes=small, **more):
    return pl.pallas_call(
        kernel,
        out_shape=out_shape,
        compiler_params=pltpu.CompilerParams(vmem_limit_bytes=vmem_bytes),
        **more,
    )


def in_vmem(count):
    return [pl.BlockSpec(memory_space=pltpu.VMEM)] * count


in_smem = pl.BlockSpec(memory_space=pltpu.SMEM)


def exchange(x, axis, groups=None):
    return lax.all_to_all(x, axis, 0, 0, axis_index_groups=groups, tiled=True)


def spread(x, axis, count, groups=None):
    return exchange(jnp.broadcast_to(x[None], (count, *x.shape)), axis, groups)


def left_half(shape):
    return lax.broadcasted_iota(jnp.int32, shape, 1) < HEAD


def swap_quarters(v):
    lane = lax.broadcasted_iota(jnp.int32, v.shape, 1)
    return jnp.where(lane % HEAD < HEAD // 2, pltpu.roll(v, LANES - 32, 1), pltpu.roll(v, 32, 1))


def head_mean(v, left):
    first = jnp.sum(jnp.where(left, v, 0.0), axis=1, keepdims=True)
    second = jnp.sum(jnp.where(left, 0.0, v), axis=1, keepdims=True)
    return jnp.where(left, first, second) * (1.0 / HEAD)


def copies_kernel(block_ref, out_ref):
    for peer in range(out_ref.shape[0]):
        out_ref[peer] = block_ref[...]


def projected(x_ref, gain_ref, w_ref):
    x = x_ref[...].astype(f32)
    scaled = x * lax.rsqrt(jnp.mean(x * x, axis=1, keepdims=True) + eps)
    normed = (scaled * gain_ref[...]).astype(bf16)
    return normed, dot(normed, w_ref[...])


def project_kernel(
    x_ref, gain_ref, w_ref, head_gain_ref, cos_ref, sin_ref, query_ref, kv_ref
):
    _, pre = projected(x_ref, gain_ref, w_ref)
    cosine, sine = cos_ref[...], sin_ref[...]
    left = left_half((x_ref.shape[0], LANES))

    def prepared(v, gain):
        v = v * lax.rsqrt(head_mean(v * v, left) + eps) * gain
        return v * cosine + swap_quarters(v) * sine

    query = prepared(pre[:, :LANES], head_gain_ref[0:1, :])
    query_ref[...] = (query * (log2e / math.sqrt(HEAD))).astype(bf16)
    pair = pre[:, LANES:]
    key = prepared(pair, head_gain_ref[1:2, :])
    both = jnp.where(left, key, pair).astype(bf16)
    for peer in range(kv_ref.shape[0]):
        kv_ref[peer] = both


def keep_kernel(x_ref, gain_ref, w_ref, normed_ref, pre_ref):
    normed_ref[...], pre_ref[...] = projected(x_ref, gain_ref, w_ref)


def earlier_spans(order_ref, list_ref, rank, core, blocks):
    count = jnp.int32(0)
    for block in range(blocks):
        list_ref[count] = jnp.int32(block)
        slot = ((block // 2) * 2 + core) * 2 + block % 2
        count = count + (order_ref[slot] < rank).astype(jnp.int32)
    return count


def block_rows(index, span):
    return pl.ds(pl.multiple_of(index * span, span), span)


def in_groups(count, size, body):
    whole = count // size

    def some(step, carry):
        body([step * size + k for k in range(size)])
        return carry

    lax.fori_loop(0, whole, some, 0)

    def one(step, carry):
        body([step])
        return carry

    lax.fori_loop(whole * size, count, one, 0)


def pieces(v, count):
    parts = []
    for _ in range(count):
        part = v.astype(bf16).astype(f32)
        parts.append(part)
        v = v - part
    return parts


def attend_kernel(order_ref, own_ref, other_ref, kv_ref, acc_ref, sent_ref, list_ref, qx_ref, sum_ref):
    me = lax.axis_index("ctx")
    core = me % 2
    span = own_ref.shape[0] // 2
    blocks = kv_ref.shape[0] // span
    left = left_half((span, LANES))
    lane = lax.broadcasted_iota(jnp.int32, (span, LANES), 1)
    for source in range(2):
        for slot in range(2):
            query = (own_ref, other_ref)[source][pl.ds(slot * span, span), :].astype(f32)
            for head in range(2):
                own = query if head == 0 else pltpu.roll(query, HEAD, 1)
                qx_ref[pl.ds(head * span, span), :] = jnp.where(left, own, 0.0).astype(bf16)
            rank = order_ref[(me + source * (1 - 2 * core)) * 2 + slot]
            count = earlier_spans(order_ref, list_ref, rank, core, blocks)

            def product(indices, mask=None):
                pair = jnp.concatenate([kv_ref[block_rows(k, span), :] for k in indices], axis=0)
                weights = jnp.exp2(dot_t(pair, qx_ref[...]))
                if mask is not None:
                    weights = jnp.where(mask, weights, 0.0)
                values = jnp.where(left_half(pair.shape), jnp.ones_like(pair), pair)
                return t_dot(values, weights.astype(bf16))

            if source == 0:
                row = lax.broadcasted_iota(jnp.int32, (span, 2 * span), 0)
                col = lax.broadcasted_iota(jnp.int32, (span, 2 * span), 1) % span
                sum_ref[...] = product([(me // 2) * 2 + slot], col >= row)
            else:
                sum_ref[...] = jnp.zeros_like(sum_ref)

            def add(steps):
                sum_ref[...] += product([list_ref[step] for step in steps])

            in_groups(count, 4, add)
            for head in range(2):
                part = pl.ds((slot * 2 + head) * span, span)
                acc = sum_ref[:, head * span : (head + 1) * span].T
                if source == 0:
                    acc_ref[part, :] = acc
                else:
                    high, middle, low = pieces(acc, 3)
                    packed = jnp.where(lane == 0, high, jnp.where(lane == 1, middle, low))
                    packed = jnp.where(lane < 3, packed, jnp.where(left, 0.0, acc))
                    sent_ref[part, :] = packed.astype(bf16)


def finish_kernel(acc_ref, recv_ref, query_ref, out_ref, attended_ref, qb_ref):
    span = query_ref.shape[0] // 2
    left = left_half((span, LANES))
    lane = lax.broadcasted_iota(jnp.int32, (span, LANES), 1)
    for slot in range(2):
        rows = pl.ds(slot * span, span)
        query = query_ref[rows, :].astype(f32)
        outs = []
        for head in range(2):
            part = pl.ds((slot * 2 + head) * span, span)
            recv = recv_ref[part, :].astype(f32)
            acc = acc_ref[part, :]
            total = jnp.sum(jnp.where(left, recv, 0.0), axis=1, keepdims=True)
            total = total + jnp.where(left, acc, pltpu.roll(acc, HEAD, 1))
            logs = jnp.log2(total)
            out = jnp.where(left, logs, (acc + recv) / total)
            out_ref[part, :] = out
            outs.append(out)
            high, middle, low = pieces(logs, 3)
            own = jnp.where(left, query if head == 0 else pltpu.roll(query, HEAD, 1), 0.0)
            own = jnp.where(lane == HEAD, -high, own)
            own = jnp.where(lane == HEAD + 1, -middle, own)
            own = jnp.where(lane == HEAD + 2, -low, own)
            qb_ref[part, :] = own.astype(bf16)
        both = jnp.where(left, pltpu.roll(outs[0], HEAD, 1), outs[1]).astype(bf16)
        for peer in range(attended_ref.shape[0]):
            attended_ref[peer, rows, :] = both


def prepare_kernel(base_ref, recv_ref, out_ref, dx_ref):
    span = base_ref.shape[0] // 2
    left = left_half((span, LANES))
    lane = lax.broadcasted_iota(jnp.int32, (span, LANES), 1)
    for slot in range(2):
        rows = pl.ds(slot * span, span)
        mixed = base_ref[rows, :]
        for peer in range(recv_ref.shape[0]):
            mixed = mixed + recv_ref[peer, rows, :].astype(f32)
        mixed = mixed.astype(bf16).astype(f32)
        for head in range(2):
            part = pl.ds((slot * 2 + head) * span, span)
            own = jnp.where(left, 0.0, pltpu.roll(mixed, HEAD, 1) if head == 0 else mixed)
            delta = jnp.sum(own * out_ref[part, :], axis=1, keepdims=True)
            high, low = pieces(delta, 2)
            own = jnp.where(lane == 0, -high, jnp.where(lane == 1, -low, own))
            dx_ref[part, :] = own.astype(bf16)


def pull_kernel(last, order_ref, kv_ref, qb_ref, dx_ref, *refs):
    if last:
        start_ref, out_ref, dq_out_ref, list_ref, qz_ref, dz_ref, dkv_ref, dq_ref = refs
        dkv_ref[...] = start_ref[...]
    else:
        dkv_ref, dq_out_ref, list_ref, qz_ref, dz_ref, dq_ref = refs
        dkv_ref[...] = jnp.zeros_like(dkv_ref)
    me = lax.axis_index("ctx")
    core = me % 2
    whose = me + 1 - 2 * core if last else me
    span = qb_ref.shape[0] // 4
    blocks = kv_ref.shape[0] // span
    left = left_half((span, LANES))
    one = jnp.ones((span, LANES), bf16)
    zero = jnp.zeros((2 * span, LANES), bf16)
    wide_left = left_half((2 * span, LANES))
    for slot in range(2):
        rows = pl.ds(slot * 2 * span, 2 * span)
        qz_ref[...] = jnp.where(wide_left, qb_ref[rows, :], zero)
        dz_ref[...] = jnp.where(wide_left, zero, dx_ref[rows, :])
        count = earlier_spans(order_ref, list_ref, order_ref[whose * 2 + slot], core, blocks)

        def product(index, mask=None):
            part = block_rows(index, span)
            pair = kv_ref[part, :]
            weights = jnp.exp2(dot_t(jnp.where(left, pair, one), qb_ref[rows, :]))
            if mask is not None:
                weights = jnp.where(mask, weights, 0.0)
            pulled = dot_t(jnp.where(left, one, pair), dx_ref[rows, :])
            score = (weights * pulled).astype(bf16)
            dkv_ref[part, :] += dot(score, qz_ref[...]) + dot(weights.astype(bf16), dz_ref[...])
            return t_dot(pair, score)

        if last:
            dq_ref[...] = jnp.zeros_like(dq_ref)
        else:
            row = lax.broadcasted_iota(jnp.int32, (span, 2 * span), 0)
            col = lax.broadcasted_iota(jnp.int32, (span, 2 * span), 1) % span
            dq_ref[...] = product((me // 2) * 2 + slot, col >= row)

        def add(steps):
            dq_ref[...] += sum(product(list_ref[step]) for step in steps)

        in_groups(count, 4, add)
        first, second = dq_ref[:, :span].T, dq_ref[:, span:].T
        both = jnp.where(left, first, pltpu.roll(second, HEAD, 1))
        dq_out_ref[pl.ds(slot * span, span), :] = both.astype(dq_out_ref.dtype)
    if last:
        factor = jnp.where(left_half((1, LANES)), 1.0 / log2e, 1.0)
        out_ref[...] = (dkv_ref[...] * factor).astype(bf16)


def rows_kernel(recv_ref, cotangent_ref, resid_ref, grad_ref, block_ref):
    width = resid_ref.shape[1]
    total = recv_ref[0].astype(f32)
    for peer in range(1, recv_ref.shape[0]):
        total = total + recv_ref[peer].astype(f32)
    grad_ref[...] = cotangent_ref[...].astype(f32) + total[:, :width]
    block_ref[...] = (resid_ref[...] + total[:, width:]).astype(bf16)


def as_rows(v):
    return jnp.concatenate([v[:, k : k + LANES] for k in range(0, v.shape[1], LANES)], axis=0)


def back_kernel(
    dq_ref, dq_recv_ref, recv_ref, pre_ref, head_gain_ref, cos_ref, sin_ref, w_ref, normed_ref,
    gain_ref, second_ref, grad_ref, pre_grad_ref, sent_ref,
):
    span = cos_ref.shape[0] // 2
    peers, _, width = sent_ref.shape
    part = 2 * span // peers
    left = left_half((span, LANES))

    def pulled(grad, pre, gain, cosine, sine):
        turned = grad * cosine - swap_quarters(grad) * sine
        factor = lax.rsqrt(head_mean(pre * pre, left) + eps)
        unit = pre * factor
        sums = jnp.sum(turned * unit, axis=0, keepdims=True)
        scaled = turned * gain
        return (scaled - unit * head_mean(scaled * unit, left)) * factor, sums

    totals = [0.0, 0.0, 0.0]
    for slot in range(2):
        rows = pl.ds(slot * span, span)
        cosine, sine = cos_ref[rows, :], sin_ref[rows, :]
        grad = (dq_ref[rows, :] + dq_recv_ref[rows, :].astype(f32)) * (1.0 / math.sqrt(HEAD))
        pair = recv_ref[0, rows, :].astype(f32)
        for peer in range(1, recv_ref.shape[0]):
            pair = pair + recv_ref[peer, rows, :].astype(f32)
        query, sums = pulled(grad, pre_ref[rows, :LANES], head_gain_ref[0:1, :], cosine, sine)
        totals[0] = totals[0] + sums
        key, sums = pulled(
            jnp.where(left, pair, 0.0), pre_ref[rows, LANES:], head_gain_ref[1:2, :], cosine, sine
        )
        totals[1] = totals[1] + sums
        pre_grad_ref[rows, :LANES] = query.astype(bf16)
        pre_grad_ref[rows, LANES:] = jnp.where(left, key, pair).astype(bf16)
        normed_part = dot_t(pre_grad_ref[rows, :], w_ref[...])
        totals[2] = totals[2] + jnp.sum(
            normed_part * normed_ref[rows, :].astype(f32), axis=0, keepdims=True
        )
        sent = normed_part.astype(bf16).reshape(peers // 2, part, width)
        sent_ref[slot * (peers // 2) : (slot + 1) * (peers // 2), :part, :] = sent
    folded = totals[0] + pltpu.roll(totals[0], HEAD, 1)
    heads = jnp.where(left_half((1, LANES)), folded, pltpu.roll(totals[1], HEAD, 1))
    sums = jnp.concatenate(
        [as_rows(totals[2] / gain_ref[...]), as_rows(second_ref[...]), jnp.broadcast_to(heads, (8, LANES))],
        axis=1,
    )
    sums = jnp.concatenate([sums, jnp.zeros_like(sums)], axis=0).astype(bf16)
    for peer in range(peers):
        sent_ref[peer, part : 2 * part, :] = grad_ref[...].astype(bf16)
        sent_ref[peer, 2 * part :, : 3 * LANES] = sums
        sent_ref[peer, 2 * part :, 3 * LANES :] = jnp.zeros((16, width - 3 * LANES), bf16)


def last_kernel(recv_ref, attended_ref, own_ref, other_ref, flat_ref):
    rows = own_ref.shape[0] - 16
    peers = recv_ref.shape[0]
    part = flat_ref.shape[0] // peers
    sums = recv_ref[0, 2 * part :, : 3 * LANES].astype(f32)
    for peer in range(1, peers):
        sums = sums + recv_ref[peer, 2 * part :, : 3 * LANES].astype(f32)
    for peer in range(peers):
        flat_ref[peer * part : (peer + 1) * part, :] = recv_ref[peer, part : 2 * part]
    by_core(
        own_ref, other_ref, slice(0, rows), slice(0, LANES), t_dot(flat_ref[...], attended_ref[...])
    )
    for target in (own_ref, other_ref):
        target[:rows, LANES:] = jnp.zeros((rows, 2 * LANES), bf16)
        target[rows:, :] = sums.astype(bf16)


def tokens_kernel(recv_ref, tokens_ref, gain_ref, resid_grad_ref, grad_ref):
    part = tokens_ref.shape[0]
    total = recv_ref[0, :part].astype(f32)
    for peer in range(1, recv_ref.shape[0]):
        total = total + recv_ref[peer, :part].astype(f32)
    x = tokens_ref[...].astype(f32)
    factor = lax.rsqrt(jnp.mean(x * x, axis=1, keepdims=True) + eps)
    unit = x * factor
    scaled = total * gain_ref[...]
    pulled = (scaled - unit * jnp.mean(scaled * unit, axis=1, keepdims=True)) * factor
    grad_ref[...] = (resid_grad_ref[...] + pulled).astype(bf16)


def by_core(own_ref, other_ref, rows, columns, value):
    core = lax.axis_index("ctx") % 2
    split = value.reshape(value.shape[0] // LANES, 2, LANES // 2, value.shape[1])
    even = split[:, 0].reshape(-1, value.shape[1])
    odd = split[:, 1].reshape(-1, value.shape[1])
    own_ref[rows, columns] = jnp.where(core == 0, even, odd).astype(bf16)
    other_ref[rows, columns] = jnp.where(core == 0, odd, even).astype(bf16)


def weights_kernel(normed_ref, pair_ref, dy_ref, hidden_ref, feed_ref):
    step = 512
    wide = pair_ref.shape[1]
    for start in range(0, normed_ref.shape[1], step):
        columns = slice(start, start + step)
        feed_ref[columns, :wide] = t_dot(normed_ref[:, columns], pair_ref[...]).astype(bf16)
        feed_ref[columns, wide:] = t_dot(dy_ref[:, columns], hidden_ref[...]).astype(bf16)


def grads_kernel(normed_ref, pre_grad_ref, own_ref, other_ref):
    rows = slice(0, own_ref.shape[0])
    wide = pre_grad_ref.shape[1]
    by_core(own_ref, other_ref, rows, slice(0, wide), t_dot(normed_ref[...], pre_grad_ref[...]))


def merge_kernel(own_ref, moved_ref, last_ref, last_moved_ref, sent_ref):
    peers = sent_ref.shape[0]
    rows = own_ref.shape[0]
    part = rows // peers

    def both(first, second):
        return (first.astype(f32) + second.astype(f32)).astype(bf16)

    grads = both(own_ref[...], moved_ref[...])
    sent_ref[:, :part, : 2 * LANES] = grads.reshape(peers, part, 2 * LANES)
    last = both(last_ref[:rows, :LANES], last_moved_ref[:rows, :LANES])
    sent_ref[:, :part, 2 * LANES :] = last.reshape(peers, part, LANES)
    sums = both(last_ref[rows:, :], last_moved_ref[rows:, :])
    for peer in range(peers):
        sent_ref[peer, part:, :] = sums


def total_kernel(recv_ref, query_ref, key_ref, value_ref, out_ref, first_ref, second_ref, heads_ref):
    part = query_ref.shape[0]
    total = recv_ref[0].astype(f32)
    for peer in range(1, recv_ref.shape[0]):
        total = total + recv_ref[peer].astype(f32)
    query_ref[...] = total[:part, :LANES]
    key_ref[...] = total[:part, LANES : LANES + HEAD]
    value_ref[...] = total[:part, LANES + HEAD : 2 * LANES]
    out_ref[...] = total[:part, 2 * LANES :]
    first_ref[...] = total[part : part + 8, :LANES]
    second_ref[...] = total[part : part + 8, LANES : 2 * LANES]
    heads_ref[...] = total[part : part + 8, 2 * LANES :]


def parts_kernel(feed_ref, gate_ref, up_ref, down_ref):
    wide = gate_ref.shape[1]
    gate_ref[...] = feed_ref[:, :wide].astype(f32)
    up_ref[...] = feed_ref[:, wide : 2 * wide].astype(f32)
    down_ref[...] = feed_ref[:, 2 * wide :].astype(f32)


def feed_kernel(
    x_ref, attended_ref, w_own_ref, w_other_ref, gain_ref, w_pair_ref, hidden_grad_ref,
    resid_ref, normed_ref, hidden_ref, pair_grad_ref, part_ref, mixed_ref, sums_ref,
    w_ref, flat_ref, all_ref,
):
    core = lax.axis_index("ctx") % 2
    mine = lax.axis_index("tp")
    width = x_ref.shape[1]
    half = width // 2
    peers, local, heads = attended_ref.shape
    w_ref[core] = w_own_ref[...]
    w_ref[1 - core] = w_other_ref[...]
    rows = 256
    wide = hidden_ref.shape[1]
    gain = gain_ref[...]
    total = jnp.zeros((1, width), f32)
    for start in range(0, local, rows):
        here = pl.ds(start, rows)
        for peer in range(peers):
            flat_ref[:, peer * heads : (peer + 1) * heads] = attended_ref[peer, here, :]
        flat = flat_ref[...]
        for side in range(2):
            columns = pl.ds(side * half, half)
            all_ref[here, columns] = x_ref[here, columns].astype(f32) + dot(flat, w_ref[side])
        resid = all_ref[here, :]
        factor = lax.rsqrt(jnp.mean(resid * resid, axis=1, keepdims=True) + eps)
        normed = (resid * factor * gain).astype(bf16)
        normed_ref[here, :] = normed
        pair = dot(normed, w_pair_ref[...])
        gate, up = pair[:, :wide], pair[:, wide:]
        hidden_grad = hidden_grad_ref[here, :]
        sigma = 1.0 / (1.0 + jnp.exp(-gate))
        swish = gate * sigma
        hidden_ref[here, :] = (swish * up).astype(bf16)
        gate_grad = (hidden_grad * up * sigma * (1.0 + gate * (1.0 - sigma))).astype(bf16)
        pair_grad_ref[here, :wide] = gate_grad
        pair_grad_ref[here, wide:] = (hidden_grad * swish).astype(bf16)
        pulled = dot_t(pair_grad_ref[here, :], w_pair_ref[...])
        unit = all_ref[here, :] * factor
        total = total + jnp.sum(pulled * unit, axis=0, keepdims=True)
        scaled = pulled * gain
        part = (scaled - unit * jnp.mean(scaled * unit, axis=1, keepdims=True)) * factor
        part = part.astype(bf16)
        part_ref[here, :] = part
        mixed = dot_t(part[:, :half], w_ref[0]) + dot_t(part[:, half:], w_ref[1])
        mixed = mixed.astype(bf16)
        for peer in range(peers):
            mixed_ref[peer, here, :] = mixed[:, peer * heads : (peer + 1) * heads]
    sums_ref[...] = total
    resid_ref[...] = all_ref[block_rows(mine, local // peers), :]


def turning(positions, span_order, me, span):
    table = positions.reshape(-1, span)
    own = [lax.dynamic_index_in_dim(table, span_order[me * 2 + k], 0, False) for k in range(2)]
    places = jnp.concatenate(own).astype(f32)
    freqs = theta ** (-(jnp.arange(HEAD // 2, dtype=f32) * 2.0 / HEAD))
    turned = places[:, None] * freqs[None, :]
    cosine, sine = jnp.cos(turned), jnp.sin(turned)
    return (
        jnp.concatenate([cosine] * 4, axis=1),
        jnp.concatenate([-sine, sine, -sine, sine], axis=1),
    )


def per_device(
    tokens, cotangent, positions, span_order, first_gain, w_query, w_key, w_value,
    query_gain, key_gain, w_out, second_gain, w_gate, w_up, w_down,
):
    ctx_count = lax.axis_size("ctx")
    tp_count = lax.axis_size("tp")
    me = lax.axis_index("ctx")
    mine = lax.axis_index("tp")
    part, width = tokens.shape
    local = part * tp_count
    span = local // 2
    half = ctx_count // 2
    heads = w_out.shape[0]
    hidden_width = w_gate.shape[1]
    same_core = [[2 * k + core for k in range(half)] for core in range(2)]
    other_core = [(k, k ^ 1) for k in range(ctx_count)]
    shape = jax.ShapeDtypeStruct
    slots = pltpu.SMEM((ctx_count + 1,), jnp.int32)

    x_all = spread(tokens, "tp", tp_count).reshape(local, width)
    w_half = lax.dynamic_slice_in_dim(w_out, (me % 2) * (width // 2), width // 2, 1)
    w_half = call(
        copies_kernel,
        shape((tp_count, heads, width // 2), bf16),
        in_specs=in_vmem(1),
        out_specs=pl.BlockSpec(memory_space=pltpu.VMEM),
        name="copies",
    )(w_half)
    w_qkv = jnp.concatenate([w_query, w_key, w_value], axis=1)
    cosine, sine = turning(positions, span_order, me, span)
    head_gain = jnp.stack(
        [jnp.concatenate([query_gain, query_gain]), jnp.concatenate([key_gain, jnp.ones_like(key_gain)])]
    )

    x_all, w_qkv, cosine, sine, head_gain = lax.optimization_barrier(
        (x_all, w_qkv, cosine, sine, head_gain)
    )
    dy_all = lax.all_gather(cotangent, "tp", axis=0, tiled=True)

    by_span = lambda rows, cols: pl.BlockSpec((rows, cols), lambda k: (k, 0))
    whole = lambda a: pl.BlockSpec(a.shape, lambda k: (0, 0))
    gain_row = first_gain.reshape(1, width)
    query, kv = call(
        project_kernel,
        (shape((local, LANES), bf16), shape((half, local, LANES), bf16)),
        grid=(2,),
        in_specs=[
            by_span(span, width), whole(gain_row), whole(w_qkv), whole(head_gain),
            by_span(span, LANES), by_span(span, LANES),
        ],
        out_specs=(
            by_span(span, LANES),
            pl.BlockSpec((half, span, LANES), lambda k: (0, k, 0)),
        ),
        name="project",
    )(x_all, gain_row, w_qkv, head_gain, cosine, sine)
    normed, pre = call(
        keep_kernel,
        (shape((local, width), bf16), shape((local, 2 * LANES), f32)),
        grid=(2,),
        in_specs=[by_span(span, width), whole(gain_row), whole(w_qkv)],
        out_specs=(by_span(span, width), by_span(span, 2 * LANES)),
        name="keep",
    )(x_all, gain_row, w_qkv)

    query_other = lax.ppermute(query, "ctx", other_core)
    kv_all = exchange(kv, "ctx", same_core).reshape(half * local, LANES)
    w_pair = jnp.concatenate([w_gate, w_up], axis=1)
    kv_all, w_pair, w_half, dy_all, normed, pre = lax.optimization_barrier(
        (kv_all, w_pair, w_half, dy_all, normed, pre)
    )
    w_out_own = exchange(w_half, "tp").reshape(width, width // 2)
    acc, sent = call(
        attend_kernel,
        (shape((2 * local, LANES), f32), shape((2 * local, LANES), bf16)),
        in_specs=[in_smem, *in_vmem(3)],
        out_specs=tuple(in_vmem(2)),
        scratch_shapes=[
            slots, pltpu.VMEM((2 * span, LANES), bf16), pltpu.VMEM((LANES, 2 * span), f32)
        ],
        cost_estimate=pl.CostEstimate(flops=8 * 10**9, bytes_accessed=2**21, transcendentals=2**23),
        name="attend",
    )(span_order, query, query_other, kv_all)
    out, attended_wide, qb = call(
        finish_kernel,
        (
            shape((2 * local, LANES), f32),
            shape((tp_count, local, LANES), bf16),
            shape((2 * local, LANES), bf16),
        ),
        in_specs=in_vmem(3),
        out_specs=tuple(in_vmem(3)),
        name="finish",
    )(acc, lax.ppermute(sent, "ctx", other_core), query)
    qb_other = lax.ppermute(qb, "ctx", other_core)
    attended_wide, w_out_own = lax.optimization_barrier((attended_wide, w_out_own))
    w_out_other = lax.ppermute(w_out_own, "ctx", other_core)

    attended_all = exchange(attended_wide, "tp")
    hidden_grad = dot_t(dy_all, w_down)
    mixed_base = dot_t(dy_all, w_out)
    resid, normed_two, hidden, pair_grad, resid_part, mixed_part, second_sum = call(
        feed_kernel,
        (
            shape((part, width), f32),
            shape((local, width), bf16),
            shape((local, hidden_width), bf16),
            shape((local, 2 * hidden_width), bf16),
            shape((local, width), bf16),
            shape((tp_count, local, heads), bf16),
            shape((1, width), f32),
        ),
        in_specs=in_vmem(7),
        out_specs=tuple(in_vmem(7)),
        scratch_shapes=[
            pltpu.VMEM((2, tp_count * heads, width // 2), bf16),
            pltpu.VMEM((256, tp_count * heads), bf16),
            pltpu.VMEM((local, width), f32),
        ],
        cost_estimate=pl.CostEstimate(flops=5 * 10**9, bytes_accessed=2**23, transcendentals=2**18),
        name="feed",
        vmem_bytes=large,
    )(
        x_all, attended_all, w_out_own, w_out_other, second_gain.reshape(1, width), w_pair,
        hidden_grad,
    )
    mixed_recv = exchange(mixed_part, "tp")

    feed = call(
        weights_kernel,
        shape((width, 3 * hidden_width), bf16),
        in_specs=in_vmem(4),
        out_specs=pl.BlockSpec(memory_space=pltpu.VMEM),
        name="weights",
        vmem_bytes=large,
    )(normed_two, pair_grad, dy_all, hidden)
    feed = lax.psum_scatter(feed, "ctx", scatter_dimension=0, tiled=True)
    down = dot(hidden, w_down).astype(bf16)
    rows_sent = jnp.concatenate([resid_part, down], axis=1).reshape(tp_count, part, 2 * width)
    rows_recv = exchange(rows_sent, "tp")

    dx = call(
        prepare_kernel,
        shape((2 * local, LANES), bf16),
        in_specs=in_vmem(3),
        out_specs=pl.BlockSpec(memory_space=pltpu.VMEM),
        name="prepare",
    )(mixed_base, mixed_recv, out)
    dx_other = lax.ppermute(dx, "ctx", other_core)
    keys_shape = (half * local, LANES)
    halves = [pltpu.VMEM((2 * span, LANES), bf16)] * 2
    pull_cost = pl.CostEstimate(flops=20 * 10**9, bytes_accessed=2**22, transcendentals=2**22)
    dkv_start, dq = call(
        partial(pull_kernel, False),
        (shape(keys_shape, f32), shape((local, LANES), f32)),
        in_specs=[in_smem, *in_vmem(3)],
        out_specs=tuple(in_vmem(2)),
        scratch_shapes=[slots, *halves, pltpu.VMEM((LANES, 2 * span), f32)],
        cost_estimate=pull_cost,
        name="pull_own",
    )(span_order, kv_all, qb, dx)
    dkv, dq_other = call(
        partial(pull_kernel, True),
        (shape(keys_shape, bf16), shape((local, LANES), bf16)),
        in_specs=[in_smem, *in_vmem(4)],
        out_specs=tuple(in_vmem(2)),
        scratch_shapes=[
            slots, *halves, pltpu.VMEM(keys_shape, f32), pltpu.VMEM((LANES, 2 * span), f32)
        ],
        cost_estimate=pull_cost,
        name="pull_other",
    )(span_order, kv_all, qb_other, dx_other, dkv_start)
    dkv, rows_recv = lax.optimization_barrier((dkv, rows_recv))
    resid_grad, block_out = call(
        rows_kernel,
        (shape((part, width), f32), shape((part, width), bf16)),
        in_specs=in_vmem(3),
        out_specs=tuple(in_vmem(2)),
        name="rows",
    )(rows_recv, cotangent, resid)
    dq_recv = lax.ppermute(dq_other, "ctx", other_core)
    dkv_recv = exchange(dkv.reshape(half, local, LANES), "ctx", same_core)

    pre_grad, sent = call(
        back_kernel,
        (shape((local, 2 * LANES), bf16), shape((tp_count, 2 * part + 16, width), bf16)),
        in_specs=in_vmem(12),
        out_specs=tuple(in_vmem(2)),
        name="back",
        vmem_bytes=large,
    )(dq, dq_recv, dkv_recv, pre, head_gain, cosine, sine, w_qkv, normed, gain_row, second_sum, resid_grad)
    recv = exchange(sent, "tp")
    grads_shape = shape((width // 2, 2 * LANES), bf16)
    grads, grads_sent = call(
        grads_kernel,
        (grads_shape, grads_shape),
        in_specs=in_vmem(2),
        out_specs=tuple(in_vmem(2)),
        name="grads",
    )(normed, pre_grad)
    grads_moved = lax.ppermute(grads_sent, "ctx", other_core)
    attended = attended_wide[0]
    recv, grads, grads_moved, attended = lax.optimization_barrier(
        (recv, grads, grads_moved, attended)
    )
    last_shape = shape((width // 2 + 16, 3 * LANES), bf16)
    last, last_sent = call(
        last_kernel,
        (last_shape, last_shape),
        in_specs=in_vmem(2),
        out_specs=tuple(in_vmem(2)),
        scratch_shapes=[pltpu.VMEM((local, width), bf16)],
        name="last",
    )(recv, attended)
    grad_tokens = call(
        tokens_kernel,
        shape((part, width), bf16),
        in_specs=in_vmem(4),
        out_specs=pl.BlockSpec(memory_space=pltpu.VMEM),
        name="tokens",
    )(recv, tokens, gain_row, resid_grad)
    sent = call(
        merge_kernel,
        shape((half, width // ctx_count + 16, 3 * LANES), bf16),
        in_specs=in_vmem(4),
        out_specs=pl.BlockSpec(memory_space=pltpu.VMEM),
        name="merge",
    )(grads, grads_moved, last, lax.ppermute(last_sent, "ctx", other_core))
    own_rows = width // ctx_count
    grad_query, grad_key, grad_value, grad_out, first_sum, second_sum, head_sums = call(
        total_kernel,
        (
            shape((own_rows, LANES), f32),
            shape((own_rows, HEAD), f32),
            shape((own_rows, HEAD), f32),
            shape((own_rows, LANES), f32),
            shape((8, LANES), f32),
            shape((8, LANES), f32),
            shape((8, LANES), f32),
        ),
        in_specs=in_vmem(1),
        out_specs=tuple(in_vmem(7)),
        name="total",
    )(exchange(sent, "ctx", same_core))
    own_shape = shape((own_rows, hidden_width), f32)
    grad_gate, grad_up, grad_down = call(
        parts_kernel,
        (own_shape, own_shape, own_shape),
        in_specs=in_vmem(1),
        out_specs=tuple(in_vmem(3)),
        name="parts",
    )(feed)
    return (
        block_out,
        grad_tokens,
        first_sum.reshape(width),
        grad_query,
        grad_key,
        grad_value,
        head_sums[0, :HEAD],
        head_sums[0, HEAD:],
        grad_out.T,
        second_sum.reshape(width),
        grad_gate,
        grad_up,
        grad_down.T,
    )


def solution(mesh):
    return jax.shard_map(
        per_device,
        mesh=mesh,
        in_specs=(
            P(("ctx", "tp"), None),
            P(("ctx", "tp"), None),
            P(),
            P(),
            P(),
            P(None, "tp"),
            P(None, "tp"),
            P(None, "tp"),
            P(),
            P(),
            P("tp", None),
            P(),
            P(None, "tp"),
            P(None, "tp"),
            P("tp", None),
        ),
        out_specs=(
            P(("ctx", "tp"), None),
            P(("ctx", "tp"), None),
            P(),
            P("ctx", "tp"),
            P("ctx", "tp"),
            P("ctx", "tp"),
            P(),
            P(),
            P("tp", "ctx"),
            P(),
            P("ctx", "tp"),
            P("ctx", "tp"),
            P("tp", "ctx"),
        ),
        check_vma=False,
    )
```
